128 devices in a mesh: tm: 8 (over z, y_hi), feat: 16 (over y_lo, x, core).
Axes of the slice: x: 4, y: 4 (y_hi: 2, y_lo: 2; y = y_hi * 2 + y_lo), z: 4, core: 2. Of those that a mesh axis runs over, the one named last changes fastest.
Arguments:
- trajectory: float32 [32768, 2048], P('tm', 'feat'), may hold values from -8 to 9
Outputs:
- moments: float32 [4, 2048, 2048], P(None, 'feat', 'tm')
The draws below stay inside these ranges and needn't reach their ends.
All inputs are finite; a program needn't handle non-finite values.
Results may differ from the reference program's by a relative error of at most 0.00035.
Values may be sent and summed in bfloat16 or wider, within the bound.
A program may use at most 128 MiB of HBM per device.

```python
import math
import jax
import jax.numpy as jnp
from jax import lax

F = 2048
FRAMES = 32768


def draw_trajectory(key, part):
    keys = jax.random.split(key, 8)
    times = jnp.arange(FRAMES, dtype=jnp.float32)[:, None]
    low = math.log(2.0 * math.pi / 3000.0)
    high = math.log(2.0 * math.pi / 24.0)
    shared_freq = jnp.exp(jax.random.uniform(keys[0], (8,), jnp.float32, low, high))
    shared_phase = jax.random.uniform(keys[1], (8,), jnp.float32, -math.pi, math.pi)
    loads = jax.random.uniform(keys[2], (8, F), jnp.float32, -0.3, 0.3)
    own_freq = jnp.exp(jax.random.uniform(keys[3], (F,), jnp.float32, low, high))
    own_phase = jax.random.uniform(keys[4], (F,), jnp.float32, -math.pi, math.pi)
    offset = jax.random.uniform(keys[5], (F,), jnp.float32, -1.0, 2.0)
    own_amp = jax.random.uniform(keys[6], (F,), jnp.float32, 0.5, 1.0)
    noise = 0.25 * jnp.clip(jax.random.normal(keys[7], (FRAMES, F), jnp.float32), -3.0, 3.0)
    values = offset[None, :] + own_amp[None, :] * jnp.sin(times * own_freq[None, :] + own_phase[None, :]) + noise
    for index in range(8):
        wave = jnp.sin(times * shared_freq[index] + shared_phase[index])
        values = values + wave * loads[index][None, :]
    return values.astype(jnp.float32)


def setup_inputs(seed: int = 0) -> dict:
    key_of = jax.random.split(jax.random.key(seed), 2)
    trajectory = draw_trajectory(jax.random.fold_in(key_of[1], 71), 0)
    return {"trajectory": trajectory}


def reference(trajectory):
    frames = trajectory.shape[0]
    mean = lax.optimization_barrier(jnp.sum(trajectory, axis=0)) / frames
    centered = (trajectory - mean).astype(jnp.bfloat16)
    outs = []
    for lag in (0, 1, 4, 16):
        part = jnp.dot(centered[:frames - lag].T, centered[lag:], preferred_element_type=jnp.float32)
        outs.append(part / jnp.sqrt(jnp.float32(frames - lag)))
    return jnp.stack(outs)
```

```python
import functools
import math

import jax
import jax.numpy as jnp
from jax import lax
from jax.experimental import pallas as pl
from jax.experimental.pallas import tpu as pltpu
from jax.sharding import PartitionSpec as P

MESH = pl.DeviceIdType.MESH
LAGS = (0, 1, 4, 16)
HALO = 16
PARTS = 4


def device(x, y, z, c):
    return (z * 2 + y // 2, ((y % 2) * 4 + x) * 2 + c)


def kernel(
    x_ref, o_ref, sums, halo, slabs, cols, lagged, prod, recv,
    s_sum, r_sum, s_halo, r_halo, s_y, r_y, s_x, r_x, s_sib, r_sib, s_out, r_out,
):
    rows = x_ref.shape[0]
    part = rows // PARTS
    tm, feat = lax.axis_index("tm"), lax.axis_index("feat")
    c, x, a = feat % 2, (feat // 2) % 4, feat // 8
    z, h = tm // 2, tm % 2
    y = h * 2 + a
    driver = c == h
    step = 1 - 2 * c
    other = 1 - c
    ahead, behind = (y + step + 4) % 4, (y - step + 4) % 4
    across = (y + 2) % 4
    left, right, far = (x + 3) % 4, (x + 1) % 4, (x + 2) % 4

    barrier = pltpu.get_barrier_semaphore()
    place = y * 4 + z
    peers = [device(x, ((place + i) % 16) // 4, (place + i) % 4, c) for i in range(1, 16)]
    peers += [device(x, y, z, other), device(left, y, z, c), device(right, y, z, c)]
    for peer in peers:
        pl.semaphore_signal(barrier, inc=1, device_id=peer, device_id_type=MESH)

    total = jnp.zeros((8, 128), jnp.float32)
    for i in range(8):
        piece = x_ref[pl.ds(i * (rows // 8), rows // 8), :]
        total = total + jnp.sum(piece.reshape(rows // 64, 8, 128), axis=0)
    sums[tm] = total
    pl.semaphore_wait(barrier, len(peers))

    def sum_copy(slot, peer, i):
        return pltpu.make_async_remote_copy(
            src_ref=sums.at[slot], dst_ref=sums.at[slot], send_sem=s_sum.at[i],
            recv_sem=r_sum.at[slot], device_id=(peer, feat), device_id_type=MESH)

    def halo_copy(peer):
        return pltpu.make_async_remote_copy(
            src_ref=x_ref.at[pl.ds(rows - HALO, HALO)], dst_ref=halo, send_sem=s_halo,
            recv_sem=r_halo, device_id=(peer, feat), device_id_type=MESH)

    for i in range(1, 8):
        sum_copy(tm, (tm + i) % 8, i).start()

    @pl.when(tm < 7)
    def _():
        halo_copy(tm + 1).start()

    @pl.when(tm > 0)
    def _():
        halo_copy(tm - 1).wait_recv()

    @pl.when(tm == 0)
    def _():
        halo[...] = jnp.zeros_like(halo)

    for i in range(1, 8):
        sum_copy((tm + i) % 8, (tm + i) % 8, i).wait_recv()
    total = sums[0]
    for i in range(1, 8):
        total = total + sums[i]
    mean = jnp.sum(total, axis=0, keepdims=True) / (8.0 * rows)

    before = jnp.where(tm > 0, halo[...] - mean, 0.0)
    slabs[y, pl.ds(0, HALO), :] = before.astype(jnp.bfloat16)

    def centre(i, carry):
        at = pl.multiple_of(i * 512, 512)
        value = x_ref[pl.ds(at, 512), :] - mean
        slabs[y, pl.ds(pl.multiple_of(at + HALO, HALO), 512), :] = value.astype(jnp.bfloat16)
        return carry

    lax.fori_loop(0, rows // 512, centre, 0)

    def y_copy(phase, j, slab, target):
        at, size = (0, part + HALO) if j == 0 else (part * j + HALO, part)
        ref = slabs.at[slab, pl.ds(at, size)]
        return pltpu.make_async_remote_copy(
            src_ref=ref, dst_ref=ref, send_sem=s_y.at[phase, j], recv_sem=r_y.at[phase, j],
            device_id=device(x, target, z, c), device_id_type=MESH)

    def half(q):
        return h if q == 0 else 1 - h

    def x_copy(q, kind, j, owner, target):
        ref = cols.at[half(q), owner, :, pl.ds(part * j, part)]
        return pltpu.make_async_remote_copy(
            src_ref=ref, dst_ref=ref, send_sem=s_x.at[q, kind, j], recv_sem=r_x.at[q, kind, j],
            device_id=device(target, y, z, c), device_id_type=MESH)

    def sib_copy(q, kind, j):
        owner = (x, left, right, far)[kind]
        ref = cols.at[half(q), owner, :, pl.ds(part * j, part)]
        return pltpu.make_async_remote_copy(
            src_ref=ref, dst_ref=ref, send_sem=s_sib.at[q, kind, j], recv_sem=r_sib.at[q, kind, j],
            device_id=device(x, y, z, other), device_id_type=MESH)

    def send_own(q, j):
        slab = y if q == 0 else across
        value = slabs[slab, pl.ds(HALO + part * j, part), :]
        cols[half(q), x, :, pl.ds(part * j, part)] = value.T
        x_copy(q, 0, j, x, right).start()
        x_copy(q, 1, j, x, left).start()
        sib_copy(q, 0, j).start()

    def pass_neighbours(q, j):
        x_copy(q, 0, j, left, left).wait_recv()
        if j < PARTS // 2:
            x_copy(q, 2, j, left, right).start()
        sib_copy(q, 1, j).start()
        x_copy(q, 1, j, right, right).wait_recv()
        if j >= PARTS // 2:
            x_copy(q, 2, j, right, left).start()
        sib_copy(q, 2, j).start()

    def pass_far(q, j):
        x_copy(q, 2, j, far, left).wait_recv()
        sib_copy(q, 3, j).start()

    def take(q, kinds):
        @pl.when(jnp.logical_not(driver))
        def _():
            for kind in kinds:
                for j in range(PARTS):
                    sib_copy(q, kind, j).wait_recv()

    def shift(slab, j):
        def body(i, carry):
            at = pl.multiple_of(part * j + i * 256, 256)
            raw = slabs[slab, pl.ds(at, 256 + HALO), :].astype(jnp.float32)
            for k, lag in enumerate(LAGS):
                moved = raw if lag == 0 else pltpu.roll(raw, lag, 0)
                lagged[slab, pl.ds(at, 256), 128 * k:128 * (k + 1)] = (
                    moved[HALO:, :].astype(jnp.bfloat16))
            return carry

        lax.fori_loop(0, part // 256, body, 0)

    def multiply(slab, owners, first):
        def body(n, carry):
            lanes = pl.ds(pl.multiple_of(n * 256, 256), 256)
            lhs = jnp.concatenate([cols[slab // 2, owner] for owner in owners], axis=0)
            out = jnp.dot(lhs, lagged[slab, :, lanes], preferred_element_type=jnp.float32)
            for m, owner in enumerate(owners):
                block = out[128 * m:128 * (m + 1)]
                if not first:
                    block = prod[slab % 2, owner, :, lanes] + block
                prod[slab % 2, owner, :, lanes] = block
            return carry

        lax.fori_loop(0, 2, body, 0)

    for j in range(PARTS):
        y_copy(0, j, y, ahead).start()

    @pl.when(driver)
    def _():
        for j in range(PARTS):
            send_own(0, j)

    for j in range(PARTS):
        shift(y, j)

    for j in range(PARTS):
        y_copy(0, j, behind, behind).wait_recv()
        y_copy(1, j, behind, ahead).start()

        @pl.when(driver)
        def _():
            pass_neighbours(0, j)

        shift(behind, j)

    for j in range(PARTS):
        y_copy(1, j, across, behind).wait_recv()

        @pl.when(driver)
        def _():
            send_own(1, j)
            pass_far(0, j)

        if j == 1:
            for i in range(PARTS):
                y_copy(2, i, y, behind).start()
        shift(across, j)

    everyone = (x, left, right, far)
    take(0, (0, 1, 2, 3))
    multiply(y, everyone, True)

    for j in range(PARTS):
        y_copy(2, j, ahead, ahead).wait_recv()

        @pl.when(driver)
        def _():
            pass_neighbours(1, j)

        shift(ahead, j)

    twin = y + 1 - 2 * a
    multiply(twin, everyone, True)

    @pl.when(driver)
    def _():
        for j in range(PARTS):
            pass_far(1, j)

    take(1, (0, 1, 2, 3))

    def out_copy(row, owner):
        ty, tz = 2 * (owner % 2) + row, 2 * a + owner // 2
        return ty, tz, pltpu.make_async_remote_copy(
            src_ref=prod.at[row, owner], dst_ref=recv.at[tm], send_sem=s_out.at[row, owner],
            recv_sem=r_out.at[tm], device_id=device(x, ty, tz, c), device_id_type=MESH)

    def send_out(row):
        for owner in range(4):
            ty, tz, copy = out_copy(row, owner)
            here = jnp.logical_and(ty == y, tz == z)

            @pl.when(here)
            def _():
                pltpu.make_async_copy(prod.at[row, owner], recv.at[tm], r_out.at[tm]).start()

            @pl.when(jnp.logical_not(here))
            def _():
                copy.start()

    multiply(across, everyone, False)
    send_out(a)
    multiply((twin + 2) % 4, everyone, False)
    send_out(1 - a)

    for cut in range(2):
        for block in range(4):
            slot = 2 * block + cut
            pltpu.make_async_copy(prod.at[0, 0], recv.at[slot], r_out.at[slot]).wait()
        for k, lag in enumerate(LAGS):
            lanes = slice(128 * k, 128 * (k + 1))
            value = recv[cut, :, lanes]
            for block in range(1, 4):
                value = value + recv[2 * block + cut, :, lanes]
            o_ref[k, :, 128 * cut:128 * (cut + 1)] = value.T * (1.0 / math.sqrt(8 * rows - lag))

    for i in range(1, 8):
        sum_copy(tm, (tm + i) % 8, i).wait_send()

    @pl.when(tm < 7)
    def _():
        halo_copy(tm + 1).wait_send()

    for j in range(PARTS):
        y_copy(0, j, y, ahead).wait_send()
        y_copy(1, j, behind, ahead).wait_send()
        y_copy(2, j, y, behind).wait_send()

    @pl.when(driver)
    def _():
        for q in range(2):
            for j in range(PARTS):
                for kind in range(3):
                    x_copy(q, kind, j, x, right).wait_send()
                for kind in range(4):
                    sib_copy(q, kind, j).wait_send()

    for row in range(2):
        for owner in range(4):
            ty, tz, copy = out_copy(row, owner)

            @pl.when(jnp.logical_not(jnp.logical_and(ty == y, tz == z)))
            def _():
                copy.wait_send()


def block(trajectory):
    rows = trajectory.shape[0]
    return pl.pallas_call(
        kernel,
        out_shape=jax.ShapeDtypeStruct((4, 128, 256), jnp.float32),
        in_specs=[pl.BlockSpec(memory_space=pltpu.VMEM)],
        out_specs=pl.BlockSpec(memory_space=pltpu.VMEM),
        scratch_shapes=[
            pltpu.VMEM((8, 8, 128), jnp.float32),
            pltpu.VMEM((HALO, 128), jnp.float32),
            pltpu.VMEM((4, rows + HALO, 128), jnp.bfloat16),
            pltpu.VMEM((2, 4, 128, rows), jnp.bfloat16),
            pltpu.VMEM((4, rows, 512), jnp.bfloat16),
            pltpu.VMEM((2, 4, 128, 512), jnp.float32),
            pltpu.VMEM((8, 128, 512), jnp.float32),
            pltpu.SemaphoreType.DMA((8,)),
            pltpu.SemaphoreType.DMA((8,)),
            pltpu.SemaphoreType.DMA,
            pltpu.SemaphoreType.DMA,
            pltpu.SemaphoreType.DMA((3, PARTS)),
            pltpu.SemaphoreType.DMA((3, PARTS)),
            pltpu.SemaphoreType.DMA((2, 3, PARTS)),
            pltpu.SemaphoreType.DMA((2, 3, PARTS)),
            pltpu.SemaphoreType.DMA((2, 4, PARTS)),
            pltpu.SemaphoreType.DMA((2, 4, PARTS)),
            pltpu.SemaphoreType.DMA((2, 4)),
            pltpu.SemaphoreType.DMA((8,)),
        ],
        compiler_params=pltpu.CompilerParams(
            collective_id=0, has_side_effects=True, vmem_limit_bytes=52 << 20),
        cost_estimate=pl.CostEstimate(
            flops=2 * rows * 128 * 2048 * 4, bytes_accessed=3 << 20, transcendentals=0),
    )(trajectory)


def solution(mesh):
    return jax.shard_map(
        block, mesh=mesh, in_specs=(P("tm", "feat"),), out_specs=P(None, "feat", "tm"),
        check_vma=False)
```

```python
import functools
import math

import jax
import jax.numpy as jnp
from jax import lax
from jax.experimental import pallas as pl
from jax.experimental.pallas import tpu as pltpu
from jax.sharding import PartitionSpec as P

MESH = pl.DeviceIdType.MESH
LAGS = (0, 1, 4, 16)
HALO = 16
PARTS = 4


def device(x, y, z, c):
    return (z * 2 + y // 2, ((y % 2) * 4 + x) * 2 + c)


def kernel(
    x_hbm, o_ref, x_ref, sums, halo, slabs, cols, lagged, prod, terms, owned, final,
    s_in, s_sum, r_sum, s_halo, r_halo, s_y, r_y, s_x, r_x, s_sib, r_sib,
    s_term, r_term, s_out, r_out,
):
    rows = x_hbm.shape[0]
    part = rows // PARTS
    tm, feat = lax.axis_index("tm"), lax.axis_index("feat")
    c, x, a = feat % 2, (feat // 2) % 4, feat // 8
    z, h = tm // 2, tm % 2
    y = h * 2 + a
    driver = c == h
    step = 1 - 2 * c
    other = 1 - c
    ahead, behind = (y + step + 4) % 4, (y - step + 4) % 4
    across = (y + 2) % 4
    left, right, far = (x + 3) % 4, (x + 1) % 4, (x + 2) % 4

    fetch = pltpu.make_async_copy(x_hbm, x_ref, s_in)
    fetch.start()

    barrier = pltpu.get_barrier_semaphore()

    def greet(*peer):
        pl.semaphore_signal(barrier, inc=1, device_id=peer, device_id_type=MESH)

    for i in range(1, 8):
        greet((tm + i) % 8, feat)
    for target in (ahead, behind):
        greet(*device(x, target, z, c))
    greet(*device(x, y, z, other))

    @pl.when(driver)
    def _():
        for target in (left, right):
            greet(*device(target, y, z, c))

    fetch.wait()
    total = jnp.zeros((8, 128), jnp.float32)
    for i in range(8):
        piece = x_ref[pl.ds(i * (rows // 8), rows // 8), :]
        total = total + jnp.sum(piece.reshape(rows // 64, 8, 128), axis=0)
    sums[tm] = total
    pl.semaphore_wait(barrier, jnp.where(driver, 12, 10))

    def sum_copy(slot, peer, i):
        return pltpu.make_async_remote_copy(
            src_ref=sums.at[slot], dst_ref=sums.at[slot], send_sem=s_sum.at[i],
            recv_sem=r_sum.at[slot], device_id=(peer, feat), device_id_type=MESH)

    def halo_copy(peer):
        return pltpu.make_async_remote_copy(
            src_ref=x_ref.at[pl.ds(rows - HALO, HALO)], dst_ref=halo, send_sem=s_halo,
            recv_sem=r_halo, device_id=(peer, feat), device_id_type=MESH)

    for i in range(1, 8):
        sum_copy(tm, (tm + i) % 8, i).start()

    @pl.when(tm < 7)
    def _():
        halo_copy(tm + 1).start()

    @pl.when(tm > 0)
    def _():
        halo_copy(tm - 1).wait_recv()

    @pl.when(tm == 0)
    def _():
        halo[...] = jnp.zeros_like(halo)

    for i in range(1, 8):
        sum_copy((tm + i) % 8, (tm + i) % 8, i).wait_recv()
    total = sums[0]
    for i in range(1, 8):
        total = total + sums[i]
    mean = jnp.sum(total, axis=0, keepdims=True) / (8.0 * rows)

    before = jnp.where(tm > 0, halo[...] - mean, 0.0)
    slabs[y, pl.ds(0, HALO), :] = before.astype(jnp.bfloat16)

    def centre(j):
        def body(i, carry):
            at = pl.multiple_of(part * j + i * 256, 256)
            value = x_ref[pl.ds(at, 256), :] - mean
            slabs[y, pl.ds(at + HALO, 256), :] = value.astype(jnp.bfloat16)
            return carry

        lax.fori_loop(0, part // 256, body, 0)

    def y_copy(phase, j, slab, target):
        at, size = (0, part + HALO) if j == 0 else (part * j + HALO, part)
        ref = slabs.at[slab, pl.ds(at, size)]
        return pltpu.make_async_remote_copy(
            src_ref=ref, dst_ref=ref, send_sem=s_y.at[phase, j], recv_sem=r_y.at[phase, j],
            device_id=device(x, target, z, c), device_id_type=MESH)

    def half(q):
        return h if q == 0 else 1 - h

    def x_copy(q, kind, j, owner, target):
        ref = cols.at[half(q), owner, :, pl.ds(part * j, part)]
        return pltpu.make_async_remote_copy(
            src_ref=ref, dst_ref=ref, send_sem=s_x.at[q, kind, j], recv_sem=r_x.at[q, kind, j],
            device_id=device(target, y, z, c), device_id_type=MESH)

    def sib_copy(q, kind, j):
        owner = (x, left, right, far)[kind]
        ref = cols.at[half(q), owner, :, pl.ds(part * j, part)]
        return pltpu.make_async_remote_copy(
            src_ref=ref, dst_ref=ref, send_sem=s_sib.at[q, kind, j], recv_sem=r_sib.at[q, kind, j],
            device_id=device(x, y, z, other), device_id_type=MESH)

    def send_own(q, j):
        slab = y if q == 0 else across
        value = slabs[slab, pl.ds(HALO + part * j, part), :]
        cols[half(q), x, :, pl.ds(part * j, part)] = value.T
        x_copy(q, 0, j, x, right).start()
        x_copy(q, 1, j, x, left).start()
        sib_copy(q, 0, j).start()

    def pass_neighbours(q, j):
        x_copy(q, 0, j, left, left).wait_recv()
        if j % 2 == 0:
            x_copy(q, 2, j, left, right).start()
        sib_copy(q, 1, j).start()
        x_copy(q, 1, j, right, right).wait_recv()
        if j % 2 == 1:
            x_copy(q, 2, j, right, left).start()
        sib_copy(q, 2, j).start()

    def pass_far(q, j):
        x_copy(q, 2, j, far, left).wait_recv()
        sib_copy(q, 3, j).start()

    def take(q, kinds):
        @pl.when(jnp.logical_not(driver))
        def _():
            for kind in kinds:
                for j in range(PARTS):
                    sib_copy(q, kind, j).wait_recv()

    def shift(slab, j):
        def body(i, carry):
            at = pl.multiple_of(part * j + i * 256, 256)
            raw = slabs[slab, pl.ds(at, 256 + HALO), :].astype(jnp.float32)
            for k, lag in enumerate(LAGS):
                moved = raw if lag == 0 else pltpu.roll(raw, lag, 0)
                lagged[slab, pl.ds(at, 256), 128 * k:128 * (k + 1)] = (
                    moved[HALO:, :].astype(jnp.bfloat16))
            return carry

        lax.fori_loop(0, part // 256, body, 0)

    def multiply(slab, owners, first):
        def body(n, carry):
            lanes = pl.ds(pl.multiple_of(n * 256, 256), 256)
            lhs = jnp.concatenate([cols[slab // 2, owner] for owner in owners], axis=0)
            out = jnp.dot(lhs, lagged[slab, :, lanes], preferred_element_type=jnp.float32)
            for m, owner in enumerate(owners):
                for i in range(2):
                    block = out[128 * m:128 * (m + 1), 128 * i:128 * (i + 1)]
                    if not first:
                        block = prod[slab % 2, owner, 2 * n + i] + block
                    prod[slab % 2, owner, 2 * n + i] = block
            return carry

        lax.fori_loop(0, 2, body, 0)

    def term_copy(row, owner, i):
        target = (z + i) % 4
        return pltpu.make_async_remote_copy(
            src_ref=prod.at[row, owner, target], dst_ref=terms.at[i - 1, row, owner],
            send_sem=s_term.at[i - 1, row, owner], recv_sem=r_term.at[i - 1, row, owner],
            device_id=device(x, y, target, c), device_id_type=MESH)

    def send_terms(row, owners):
        for owner in owners:
            for i in (2, 1, 3):
                term_copy(row, owner, i).start()

    def out_copy(row, owner):
        ty, tz = 2 * (owner % 2) + row, 2 * a + owner // 2
        copy = pltpu.make_async_remote_copy(
            src_ref=owned.at[row, owner], dst_ref=final.at[tm], send_sem=s_out.at[row, owner],
            recv_sem=r_out.at[tm], device_id=device(x, ty, tz, c), device_id_type=MESH)
        return jnp.logical_and(ty == y, tz == z), copy

    def send_out(row, owners):
        for owner in owners:
            value = prod[row, owner, z]
            for i in range(1, 4):
                term_copy(row, owner, i).wait_recv()
                value = value + terms[i - 1, row, owner]
            owned[row, owner] = value
            here, copy = out_copy(row, owner)

            @pl.when(here)
            def _():
                pltpu.make_async_copy(owned.at[row, owner], final.at[tm], r_out.at[tm]).start()

            @pl.when(jnp.logical_not(here))
            def _():
                copy.start()

    everyone = (x, left, right, far)
    twin = y + 1 - 2 * a
    opposite = (twin + 2) % 4

    for j in range(PARTS):
        centre(j)
        if j < 2:
            y_copy(0, j, y, ahead).start()

        @pl.when(driver)
        def _():
            send_own(0, j)

    for j in range(PARTS):
        shift(y, j)

    for j in range(PARTS):
        y_copy(0, j, behind, behind).wait_recv()
        y_copy(1, j, behind, ahead).start()
        if j + 2 < PARTS:
            y_copy(0, j + 2, y, ahead).start()

        @pl.when(driver)
        def _():
            pass_neighbours(0, j)

        shift(behind, j)

    for j in range(PARTS):
        y_copy(1, j, across, behind).wait_recv()

        @pl.when(driver)
        def _():
            send_own(1, j)
            pass_far(0, j)

        if j == 2:
            for i in range(PARTS):
                y_copy(2, i, y, behind).start()
        shift(across, j)

    take(0, (0, 1, 2, 3))
    multiply(y, everyone, True)
    take(1, (0,))
    multiply(across, (x,), False)
    send_terms(a, (x,))

    for j in range(PARTS):
        y_copy(2, j, ahead, ahead).wait_recv()

        @pl.when(driver)
        def _():
            pass_neighbours(1, j)

        shift(ahead, j)

    take(1, (1, 2))
    multiply(across, (left, right), False)
    send_terms(a, (left, right))
    multiply(twin, everyone, True)
    multiply(opposite, (left, right), False)
    send_terms(1 - a, (left, right))

    @pl.when(driver)
    def _():
        for j in range(PARTS):
            pass_far(1, j)

    take(1, (3,))
    multiply(across, (far,), False)
    send_terms(a, (far,))
    multiply(opposite, (far, x), False)
    send_terms(1 - a, (far, x))
    send_out(a, (x, left, right))
    send_out(1 - a, (left, right))
    send_out(a, (far,))
    send_out(1 - a, (far, x))

    for cut in range(2):
        for k, lag in enumerate(LAGS):
            slot = 2 * k + cut
            pltpu.make_async_copy(owned.at[0, 0], final.at[slot], r_out.at[slot]).wait()
            o_ref[k, :, 128 * cut:128 * (cut + 1)] = (
                final[slot].T * (1.0 / math.sqrt(8 * rows - lag)))

    for i in range(1, 8):
        sum_copy(tm, (tm + i) % 8, i).wait_send()

    @pl.when(tm < 7)
    def _():
        halo_copy(tm + 1).wait_send()

    for j in range(PARTS):
        y_copy(0, j, y, ahead).wait_send()
        y_copy(1, j, behind, ahead).wait_send()
        y_copy(2, j, y, behind).wait_send()

    @pl.when(driver)
    def _():
        for q in range(2):
            for j in range(PARTS):
                for kind in range(3):
                    x_copy(q, kind, j, x, right).wait_send()
                for kind in range(4):
                    sib_copy(q, kind, j).wait_send()

    for row in range(2):
        for owner in range(4):
            for i in range(1, 4):
                term_copy(row, owner, i).wait_send()
            here, copy = out_copy(row, owner)

            @pl.when(jnp.logical_not(here))
            def _():
                copy.wait_send()


def block(trajectory):
    rows = trajectory.shape[0]
    return pl.pallas_call(
        kernel,
        out_shape=jax.ShapeDtypeStruct((4, 128, 256), jnp.float32),
        in_specs=[pl.BlockSpec(memory_space=pl.ANY)],
        out_specs=pl.BlockSpec(memory_space=pltpu.VMEM),
        scratch_shapes=[
            pltpu.VMEM((rows, 128), jnp.float32),
            pltpu.VMEM((8, 8, 128), jnp.float32),
            pltpu.VMEM((HALO, 128), jnp.float32),
            pltpu.VMEM((4, rows + HALO, 128), jnp.bfloat16),
            pltpu.VMEM((2, 4, 128, rows), jnp.bfloat16),
            pltpu.VMEM((4, rows, 512), jnp.bfloat16),
            pltpu.VMEM((2, 4, 4, 128, 128), jnp.float32),
            pltpu.VMEM((3, 2, 4, 128, 128), jnp.float32),
            pltpu.VMEM((2, 4, 128, 128), jnp.float32),
            pltpu.VMEM((8, 128, 128), jnp.float32),
            pltpu.SemaphoreType.DMA,
            pltpu.SemaphoreType.DMA((8,)),
            pltpu.SemaphoreType.DMA((8,)),
            pltpu.SemaphoreType.DMA,
            pltpu.SemaphoreType.DMA,
            pltpu.SemaphoreType.DMA((3, PARTS)),
            pltpu.SemaphoreType.DMA((3, PARTS)),
            pltpu.SemaphoreType.DMA((2, 3, PARTS)),
            pltpu.SemaphoreType.DMA((2, 3, PARTS)),
            pltpu.SemaphoreType.DMA((2, 4, PARTS)),
            pltpu.SemaphoreType.DMA((2, 4, PARTS)),
            pltpu.SemaphoreType.DMA((3, 2, 4)),
            pltpu.SemaphoreType.DMA((3, 2, 4)),
            pltpu.SemaphoreType.DMA((2, 4)),
            pltpu.SemaphoreType.DMA((8,)),
        ],
        compiler_params=pltpu.CompilerParams(
            collective_id=0, has_side_effects=True, vmem_limit_bytes=52 << 20),
        cost_estimate=pl.CostEstimate(
            flops=2 * rows * 128 * 2048 * 4, bytes_accessed=3 << 20, transcendentals=0),
    )(trajectory)


def solution(mesh):
    return jax.shard_map(
        block, mesh=mesh, in_specs=(P("tm", "feat"),), out_specs=P(None, "feat", "tm"),
        check_vma=False)
```

```python
import functools
import math

import jax
import jax.numpy as jnp
from jax import lax
from jax.experimental import pallas as pl
from jax.experimental.pallas import tpu as pltpu
from jax.sharding import PartitionSpec as P

MESH = pl.DeviceIdType.MESH
LAGS = (0, 1, 4, 16)
HALO = 16
PARTS = 4


def device(x, y, z, c):
    return (z * 2 + y // 2, ((y % 2) * 4 + x) * 2 + c)


def kernel(
    x_hbm, o_ref, x_ref, sums, halo, slabs, cols, lagged, prod, terms, owned,
    s_in, s_sum, r_sum, s_halo, r_halo, s_y, r_y, s_x, r_x, s_sib, r_sib,
    s_term, r_term, s_out, r_out,
):
    rows = x_hbm.shape[0]
    part = rows // PARTS
    tm, feat = lax.axis_index("tm"), lax.axis_index("feat")
    c, x, a = feat % 2, (feat // 2) % 4, feat // 8
    z, h = tm // 2, tm % 2
    y = h * 2 + a
    driver = c == h
    other = 1 - c
    twin = y + 1 - 2 * a
    opposite, across = (twin + 2) % 4, (y + 2) % 4
    left, right, far = (x + 3) % 4, (x + 1) % 4, (x + 2) % 4

    fetch = pltpu.make_async_copy(x_hbm, x_ref, s_in)
    fetch.start()

    barrier = pltpu.get_barrier_semaphore()

    def greet(*peer):
        pl.semaphore_signal(barrier, inc=1, device_id=peer, device_id_type=MESH)

    for i in range(1, 8):
        greet((tm + i) % 8, feat)
    for target in (twin, opposite):
        greet(*device(x, target, z, c))
    greet(*device(x, y, z, other))

    @pl.when(driver)
    def _():
        for target in (left, right):
            greet(*device(target, y, z, c))

    fetch.wait()
    total = jnp.zeros((8, 128), jnp.float32)
    for i in range(8):
        piece = x_ref[pl.ds(i * (rows // 8), rows // 8), :]
        total = total + jnp.sum(piece.reshape(rows // 64, 8, 128), axis=0)
    sums[tm] = total
    pl.semaphore_wait(barrier, jnp.where(driver, 12, 10))

    def sum_copy(slot, peer, i):
        return pltpu.make_async_remote_copy(
            src_ref=sums.at[slot], dst_ref=sums.at[slot], send_sem=s_sum.at[i],
            recv_sem=r_sum.at[slot], device_id=(peer, feat), device_id_type=MESH)

    def halo_copy(peer):
        return pltpu.make_async_remote_copy(
            src_ref=x_ref.at[pl.ds(rows - HALO, HALO)], dst_ref=halo, send_sem=s_halo,
            recv_sem=r_halo, device_id=(peer, feat), device_id_type=MESH)

    for i in range(1, 8):
        sum_copy(tm, (tm + i) % 8, i).start()

    @pl.when(tm < 7)
    def _():
        halo_copy(tm + 1).start()

    @pl.when(tm > 0)
    def _():
        halo_copy(tm - 1).wait_recv()

    @pl.when(tm == 0)
    def _():
        halo[...] = jnp.zeros_like(halo)

    for i in range(1, 8):
        sum_copy((tm + i) % 8, (tm + i) % 8, i).wait_recv()
    total = sums[0]
    for i in range(1, 8):
        total = total + sums[i]
    mean = jnp.sum(total, axis=0, keepdims=True) / (8.0 * rows)

    before = jnp.where(tm > 0, halo[...] - mean, 0.0)
    slabs[y, pl.ds(0, HALO), :] = before.astype(jnp.bfloat16)

    def centre(j):
        def body(i, carry):
            at = pl.multiple_of(part * j + i * 256, 256)
            value = x_ref[pl.ds(at, 256), :] - mean
            slabs[y, pl.ds(at + HALO, 256), :] = value.astype(jnp.bfloat16)
            return carry

        lax.fori_loop(0, part // 256, body, 0)

    def y_copy(kind, group, j, slab, target):
        at, size = (0, part + HALO) if j == 0 else (part * j + HALO, part)
        ref = slabs.at[slab, pl.ds(at, size)]
        return pltpu.make_async_remote_copy(
            src_ref=ref, dst_ref=ref, send_sem=s_y.at[group, j], recv_sem=r_y.at[kind, j],
            device_id=device(x, target, z, c), device_id_type=MESH)

    def arrived(kind, j):
        slab = (twin, opposite, across)[kind]
        y_copy(kind, 0, j, slab, twin).wait_recv()

    def half(q):
        return h if q == 0 else 1 - h

    def x_copy(q, kind, j, owner, target):
        ref = cols.at[half(q), owner, :, pl.ds(part * j, part)]
        return pltpu.make_async_remote_copy(
            src_ref=ref, dst_ref=ref, send_sem=s_x.at[q, kind, j], recv_sem=r_x.at[q, kind, j],
            device_id=device(target, y, z, c), device_id_type=MESH)

    def sib_copy(q, kind, j):
        owner = (x, left, right, far)[kind]
        ref = cols.at[half(q), owner, :, pl.ds(part * j, part)]
        return pltpu.make_async_remote_copy(
            src_ref=ref, dst_ref=ref, send_sem=s_sib.at[q, kind, j], recv_sem=r_sib.at[q, kind, j],
            device_id=device(x, y, z, other), device_id_type=MESH)

    def send_own(q, j):
        slab = y if q == 0 else across
        value = slabs[slab, pl.ds(HALO + part * j, part), :]
        cols[half(q), x, :, pl.ds(part * j, part)] = value.T
        x_copy(q, 0, j, x, right).start()
        x_copy(q, 1, j, x, left).start()
        sib_copy(q, 0, j).start()

    def neighbours(q, j):
        x_copy(q, 0, j, left, left).wait_recv()
        sib_copy(q, 1, j).start()
        x_copy(q, 1, j, right, right).wait_recv()
        sib_copy(q, 2, j).start()

    def pass_on(q, j):
        if j % 2 == 0:
            x_copy(q, 2, j, left, right).start()
        else:
            x_copy(q, 2, j, right, left).start()

    def pass_far(q, j):
        x_copy(q, 2, j, far, left).wait_recv()
        sib_copy(q, 3, j).start()

    def take(q, kinds):
        for kind in kinds:
            for j in range(PARTS):
                sib_copy(q, kind, j).wait_recv()

    def shift(slab, j):
        def body(i, carry):
            at = pl.multiple_of(part * j + i * 256, 256)
            raw = slabs[slab, pl.ds(at, 256 + HALO), :].astype(jnp.float32)
            for k, lag in enumerate(LAGS):
                moved = raw if lag == 0 else pltpu.roll(raw, lag, 0)
                lagged[slab, pl.ds(at, 256), 128 * k:128 * (k + 1)] = (
                    moved[HALO:, :].astype(jnp.bfloat16))
            return carry

        lax.fori_loop(0, part // 256, body, 0)

    def multiply(slab, owners, first):
        def body(n, carry):
            lanes = pl.ds(pl.multiple_of(n * 256, 256), 256)
            lhs = jnp.concatenate([cols[slab // 2, owner] for owner in owners], axis=0)
            out = jnp.dot(lhs, lagged[slab, :, lanes], preferred_element_type=jnp.float32)
            for m, owner in enumerate(owners):
                for i in range(2):
                    block = out[128 * m:128 * (m + 1), 128 * i:128 * (i + 1)]
                    if not first:
                        block = prod[slab % 2, owner, 2 * n + i] + block
                    prod[slab % 2, owner, 2 * n + i] = block
            return carry

        lax.fori_loop(0, 2, body, 0)

    def term_copy(row, owner, i):
        target = (z + i) % 4
        return pltpu.make_async_remote_copy(
            src_ref=prod.at[row, owner, target], dst_ref=terms.at[i - 1, row, owner],
            send_sem=s_term.at[i - 1, row, owner], recv_sem=r_term.at[i - 1, row, owner],
            device_id=device(x, y, target, c), device_id_type=MESH)

    def send_terms(row, owners):
        for owner in owners:
            for i in (2, 1, 3):
                term_copy(row, owner, i).start()

    def out_copy(row, owner):
        ty, tz = 2 * (owner % 2) + row, 2 * a + owner // 2
        place = o_ref.at[z, :, pl.ds(pl.multiple_of(h * 128, 128), 128)]
        copy = pltpu.make_async_remote_copy(
            src_ref=owned.at[row, owner], dst_ref=place, send_sem=s_out.at[row, owner],
            recv_sem=r_out.at[tm], device_id=device(x, ty, tz, c), device_id_type=MESH)
        return jnp.logical_and(ty == y, tz == z), place, copy

    scale = jnp.float32(1.0 / math.sqrt(8 * rows))
    for k in range(1, 4):
        scale = jnp.where(z == k, jnp.float32(1.0 / math.sqrt(8 * rows - LAGS[k])), scale)

    def send_out(row, owners):
        for owner in owners:
            value = prod[row, owner, z]
            for i in range(1, 4):
                term_copy(row, owner, i).wait_recv()
                value = value + terms[i - 1, row, owner]
            owned[row, owner] = value.T * scale
            here, place, copy = out_copy(row, owner)

            @pl.when(here)
            def _():
                pltpu.make_async_copy(owned.at[row, owner], place, r_out.at[tm]).start()

            @pl.when(jnp.logical_not(here))
            def _():
                copy.start()

    close = (x, left, right)

    @pl.when(driver)
    def _():
        for j in range(PARTS):
            centre(j)
            if j < 2:
                y_copy(1, 0, j, y, opposite).start()
            send_own(0, j)
        for j in range(PARTS):
            shift(y, j)
        neighbours(0, 0)
        pass_on(0, 0)
        neighbours(0, 1)
        pass_on(0, 1)
        neighbours(0, 2)
        for j in range(PARTS):
            arrived(2, j)
            send_own(1, j)
            if j == 0:
                neighbours(0, 3)
            if j == 1:
                y_copy(1, 0, 2, y, opposite).start()
                y_copy(1, 0, 3, y, opposite).start()
            if j >= 2:
                pass_far(0, j - 2)
            shift(across, j)
        pass_on(0, 2)
        pass_on(0, 3)
        for j in range(PARTS):
            y_copy(0, 1, j, y, twin).start()
        multiply(y, close, True)
        multiply(across, (x,), False)
        send_terms(a, (x,))
        for j in range(PARTS):
            neighbours(1, j)
            pass_on(1, j)
        multiply(across, (left, right), False)
        send_terms(a, (left, right))
        pass_far(0, 2)
        pass_far(0, 3)
        multiply(y, (far,), True)
        for j in range(PARTS):
            arrived(0, j)
            shift(twin, j)
            if j == 1:
                pass_far(1, 0)
                pass_far(1, 1)
        multiply(twin, close + (far,), True)
        pass_far(1, 2)
        pass_far(1, 3)
        multiply(across, (far,), False)
        send_terms(a, (far,))
        for j in range(PARTS):
            arrived(1, j)
            shift(opposite, j)
        multiply(opposite, close + (far,), False)
        send_terms(1 - a, close + (far,))
        send_out(a, close + (far,))
        send_out(1 - a, close + (far,))

    @pl.when(jnp.logical_not(driver))
    def _():
        for j in range(PARTS):
            centre(j)
            y_copy(0, 0, j, y, twin).start()
        for j in range(PARTS):
            shift(y, j)
        for j in range(PARTS):
            arrived(0, j)
            y_copy(2, 2, j, twin, opposite).start()
            if j < 2:
                arrived(1, j)
                y_copy(2, 3, j, opposite, twin).start()
                shift(opposite, j)
            shift(twin, j)
        take(0, (0, 1, 2))
        multiply(y, close, True)
        multiply(twin, close, True)
        for j in range(2, PARTS):
            arrived(1, j)
            y_copy(2, 3, j, opposite, twin).start()
            if j == 2:
                for i in range(PARTS):
                    y_copy(1, 1, i, y, opposite).start()
            shift(opposite, j)
        take(1, (0,))
        multiply(opposite, (x,), False)
        send_terms(1 - a, (x,))
        for j in range(2):
            arrived(2, j)
            shift(across, j)
        take(1, (1, 2))
        multiply(opposite, (left, right), False)
        send_terms(1 - a, (left, right))
        take(0, (3,))
        multiply(y, (far,), True)
        multiply(twin, (far,), True)
        for j in range(2, PARTS):
            arrived(2, j)
            shift(across, j)
        multiply(across, close, False)
        send_terms(a, close)
        take(1, (3,))
        multiply(opposite, (far,), False)
        send_terms(1 - a, (far,))
        multiply(across, (far,), False)
        send_terms(a, (far,))
        send_out(1 - a, close)
        send_out(a, close)
        send_out(1 - a, (far,))
        send_out(a, (far,))

    for slot in range(8):
        place = o_ref.at[slot // 2, :, pl.ds(128 * (slot % 2), 128)]
        pltpu.make_async_copy(owned.at[0, 0], place, r_out.at[slot]).wait()

    for i in range(1, 8):
        sum_copy(tm, (tm + i) % 8, i).wait_send()

    @pl.when(tm < 7)
    def _():
        halo_copy(tm + 1).wait_send()

    for j in range(PARTS):
        for group in range(2):
            y_copy(0, group, j, y, twin).wait_send()

    @pl.when(driver)
    def _():
        for q in range(2):
            for j in range(PARTS):
                for kind in range(3):
                    x_copy(q, kind, j, x, right).wait_send()
                for kind in range(4):
                    sib_copy(q, kind, j).wait_send()

    @pl.when(jnp.logical_not(driver))
    def _():
        for j in range(PARTS):
            for group in range(2, 4):
                y_copy(0, group, j, y, twin).wait_send()

    for row in range(2):
        for owner in range(4):
            for i in range(1, 4):
                term_copy(row, owner, i).wait_send()
            here, place, copy = out_copy(row, owner)

            @pl.when(jnp.logical_not(here))
            def _():
                copy.wait_send()


def block(trajectory):
    rows = trajectory.shape[0]
    return pl.pallas_call(
        kernel,
        out_shape=jax.ShapeDtypeStruct((4, 128, 256), jnp.float32),
        in_specs=[pl.BlockSpec(memory_space=pl.ANY)],
        out_specs=pl.BlockSpec(memory_space=pltpu.VMEM),
        scratch_shapes=[
            pltpu.VMEM((rows, 128), jnp.float32),
            pltpu.VMEM((8, 8, 128), jnp.float32),
            pltpu.VMEM((HALO, 128), jnp.float32),
            pltpu.VMEM((4, rows + HALO, 128), jnp.bfloat16),
            pltpu.VMEM((2, 4, 128, rows), jnp.bfloat16),
            pltpu.VMEM((4, rows, 512), jnp.bfloat16),
            pltpu.VMEM((2, 4, 4, 128, 128), jnp.float32),
            pltpu.VMEM((3, 2, 4, 128, 128), jnp.float32),
            pltpu.VMEM((2, 4, 128, 128), jnp.float32),
            pltpu.SemaphoreType.DMA,
            pltpu.SemaphoreType.DMA((8,)),
            pltpu.SemaphoreType.DMA((8,)),
            pltpu.SemaphoreType.DMA,
            pltpu.SemaphoreType.DMA,
            pltpu.SemaphoreType.DMA((4, PARTS)),
            pltpu.SemaphoreType.DMA((3, PARTS)),
            pltpu.SemaphoreType.DMA((2, 3, PARTS)),
            pltpu.SemaphoreType.DMA((2, 3, PARTS)),
            pltpu.SemaphoreType.DMA((2, 4, PARTS)),
            pltpu.SemaphoreType.DMA((2, 4, PARTS)),
            pltpu.SemaphoreType.DMA((3, 2, 4)),
            pltpu.SemaphoreType.DMA((3, 2, 4)),
            pltpu.SemaphoreType.DMA((2, 4)),
            pltpu.SemaphoreType.DMA((8,)),
        ],
        compiler_params=pltpu.CompilerParams(
            collective_id=0, has_side_effects=True, vmem_limit_bytes=52 << 20),
        cost_estimate=pl.CostEstimate(
            flops=2 * rows * 128 * 2048 * 4, bytes_accessed=3 << 20, transcendentals=0),
    )(trajectory)


def solution(mesh):
    return jax.shard_map(
        block, mesh=mesh, in_specs=(P("tm", "feat"),), out_specs=P(None, "feat", "tm"),
        check_vma=False)
```

```python
import functools
import math

import jax
import jax.numpy as jnp
from jax import lax
from jax.experimental import pallas as pl
from jax.experimental.pallas import tpu as pltpu
from jax.sharding import PartitionSpec as P

MESH = pl.DeviceIdType.MESH
LAGS = (0, 1, 4, 16)
HALO = 16
PARTS = 4


def device(x, y, z, c):
    return (z * 2 + (y >> 1), ((y & 1) * 4 + x) * 2 + c)


def kernel(
    x_hbm, o_ref, x_ref, sums, halo, slabs, cols, lagged, prod, terms, owned,
    s_in, s_sum, r_sum, s_halo, r_halo, s_y, r_y, s_x, r_x, s_sib, r_sib,
    s_term, r_term, s_out, r_out,
):
    rows = x_hbm.shape[0]
    part = rows // PARTS
    tm, feat = lax.axis_index("tm"), lax.axis_index("feat")
    c, x, a = feat & 1, (feat >> 1) & 3, feat >> 3
    z, h = tm >> 1, tm & 1
    y = h * 2 + a
    driver = c == h
    other = 1 - c
    twin = y + 1 - 2 * a
    opposite, across = (twin + 2) & 3, (y + 2) & 3
    left, right, far = (x + 3) & 3, (x + 1) & 3, (x + 2) & 3

    fetch = pltpu.make_async_copy(x_hbm, x_ref, s_in)
    fetch.start()

    barrier = pltpu.get_barrier_semaphore()

    def greet(*peer):
        pl.semaphore_signal(barrier, inc=1, device_id=peer, device_id_type=MESH)

    for i in range(1, 8):
        greet((tm + i) & 7, feat)
    for target in (twin, opposite):
        greet(*device(x, target, z, c))
    greet(*device(x, y, z, other))

    @pl.when(driver)
    def _():
        for target in (left, right):
            greet(*device(target, y, z, c))

    fetch.wait()
    total = jnp.zeros((8, 128), jnp.float32)
    for i in range(8):
        piece = x_ref[pl.ds(i * (rows // 8), rows // 8), :]
        total = total + jnp.sum(piece.reshape(rows // 64, 8, 128), axis=0)
    sums[tm] = total
    pl.semaphore_wait(barrier, jnp.where(driver, 12, 10))

    def sum_copy(slot, peer, i):
        return pltpu.make_async_remote_copy(
            src_ref=sums.at[slot], dst_ref=sums.at[slot], send_sem=s_sum.at[i],
            recv_sem=r_sum.at[slot], device_id=(peer, feat), device_id_type=MESH)

    def halo_copy(peer):
        return pltpu.make_async_remote_copy(
            src_ref=x_ref.at[pl.ds(rows - HALO, HALO)], dst_ref=halo, send_sem=s_halo,
            recv_sem=r_halo, device_id=(peer, feat), device_id_type=MESH)

    for i in range(1, 8):
        sum_copy(tm, (tm + i) & 7, i).start()

    @pl.when(tm < 7)
    def _():
        halo_copy(tm + 1).start()

    @pl.when(tm > 0)
    def _():
        halo_copy(tm - 1).wait_recv()

    @pl.when(tm == 0)
    def _():
        halo[...] = jnp.zeros_like(halo)

    for i in range(1, 8):
        sum_copy((tm + i) & 7, (tm + i) & 7, i).wait_recv()
    total = sums[0]
    for i in range(1, 8):
        total = total + sums[i]
    mean = jnp.sum(total, axis=0, keepdims=True) / (8.0 * rows)

    before = jnp.where(tm > 0, halo[...] - mean, 0.0)
    slabs[y, pl.ds(0, HALO), :] = before.astype(jnp.bfloat16)

    def centre(j):
        def body(i, carry):
            at = pl.multiple_of(part * j + i * 256, 256)
            value = x_ref[pl.ds(at, 256), :] - mean
            slabs[y, pl.ds(at + HALO, 256), :] = value.astype(jnp.bfloat16)
            return carry

        lax.fori_loop(0, part // 256, body, 0)

    def y_copy(kind, group, j, slab, target):
        at, size = (0, part + HALO) if j == 0 else (part * j + HALO, part)
        ref = slabs.at[slab, pl.ds(at, size)]
        return pltpu.make_async_remote_copy(
            src_ref=ref, dst_ref=ref, send_sem=s_y.at[group, j], recv_sem=r_y.at[kind, j],
            device_id=device(x, target, z, c), device_id_type=MESH)

    def arrived(kind, j):
        slab = (twin, opposite, across)[kind]
        y_copy(kind, 0, j, slab, twin).wait_recv()

    def half(q):
        return h if q == 0 else 1 - h

    def x_copy(q, kind, j, owner, target):
        ref = cols.at[half(q), owner, :, pl.ds(part * j, part)]
        return pltpu.make_async_remote_copy(
            src_ref=ref, dst_ref=ref, send_sem=s_x.at[q, kind, j], recv_sem=r_x.at[q, kind, j],
            device_id=device(target, y, z, c), device_id_type=MESH)

    def sib_copy(q, kind, j):
        owner = (x, left, right, far)[kind]
        ref = cols.at[half(q), owner, :, pl.ds(2 * part * j, 2 * part)]
        return pltpu.make_async_remote_copy(
            src_ref=ref, dst_ref=ref, send_sem=s_sib.at[q, kind, j], recv_sem=r_sib.at[q, kind, j],
            device_id=device(x, y, z, other), device_id_type=MESH)

    def send_own(q, j):
        slab = y if q == 0 else across
        value = slabs[slab, pl.ds(HALO + part * j, part), :]
        cols[half(q), x, :, pl.ds(part * j, part)] = value.T
        x_copy(q, 0, j, x, right).start()
        x_copy(q, 1, j, x, left).start()
        if j % 2:
            sib_copy(q, 0, j // 2).start()

    def neighbours(q, j):
        x_copy(q, 0, j, left, left).wait_recv()
        x_copy(q, 1, j, right, right).wait_recv()
        if j % 2:
            sib_copy(q, 1, j // 2).start()
            sib_copy(q, 2, j // 2).start()

    def pass_on(q, j):
        if j % 2 == 0:
            x_copy(q, 2, j, left, right).start()
        else:
            x_copy(q, 2, j, right, left).start()

    def pass_far(q, j):
        x_copy(q, 2, j, far, left).wait_recv()
        if j % 2:
            sib_copy(q, 3, j // 2).start()

    def take(q, kinds):
        for kind in kinds:
            for j in range(PARTS // 2):
                sib_copy(q, kind, j).wait_recv()

    def shift(slab, j):
        def body(i, carry):
            at = pl.multiple_of(part * j + i * 256, 256)
            raw = slabs[slab, pl.ds(at, 256 + HALO), :].astype(jnp.float32)
            for k, lag in enumerate(LAGS):
                moved = raw if lag == 0 else pltpu.roll(raw, lag, 0)
                lagged[slab, pl.ds(at, 256), 128 * k:128 * (k + 1)] = (
                    moved[HALO:, :].astype(jnp.bfloat16))
            return carry

        lax.fori_loop(0, part // 256, body, 0)

    def multiply(slab, owners, first, parts=None):
        at = pl.ds(0, rows) if parts is None else pl.ds(part * parts[0], part * len(parts))

        def body(n, carry):
            lanes = pl.ds(pl.multiple_of(n * 256, 256), 256)
            lhs = jnp.concatenate([cols[slab >> 1, owner, :, at] for owner in owners], axis=0)
            out = jnp.dot(lhs, lagged[slab, at, lanes], preferred_element_type=jnp.float32)
            for m, owner in enumerate(owners):
                for i in range(2):
                    block = out[128 * m:128 * (m + 1), 128 * i:128 * (i + 1)]
                    if not first:
                        block = prod[slab & 1, owner, 2 * n + i] + block
                    prod[slab & 1, owner, 2 * n + i] = block
            return carry

        lax.fori_loop(0, 2, body, 0)

    def term_copy(row, owner, i):
        target = (z + i) & 3
        return pltpu.make_async_remote_copy(
            src_ref=prod.at[row, owner, target], dst_ref=terms.at[i - 1, row, owner],
            send_sem=s_term.at[i - 1, row, owner], recv_sem=r_term.at[i - 1, row, owner],
            device_id=device(x, y, target, c), device_id_type=MESH)

    def send_terms(row, owners):
        for owner in owners:
            for i in (2, 1, 3):
                term_copy(row, owner, i).start()

    def out_copy(row, owner):
        ty, tz = 2 * (owner & 1) + row, 2 * a + (owner >> 1)
        place = o_ref.at[z, :, pl.ds(pl.multiple_of(h * 128, 128), 128)]
        copy = pltpu.make_async_remote_copy(
            src_ref=owned.at[row, owner], dst_ref=place, send_sem=s_out.at[row, owner],
            recv_sem=r_out.at[tm], device_id=device(x, ty, tz, c), device_id_type=MESH)
        return jnp.logical_and(ty == y, tz == z), place, copy

    scale = jnp.float32(1.0 / math.sqrt(8 * rows))
    for k in range(1, 4):
        scale = jnp.where(z == k, jnp.float32(1.0 / math.sqrt(8 * rows - LAGS[k])), scale)

    def send_out(row, owners):
        for owner in owners:
            value = prod[row, owner, z]
            for i in range(1, 4):
                term_copy(row, owner, i).wait_recv()
                value = value + terms[i - 1, row, owner]
            owned[row, owner] = value.T * scale
            here, place, copy = out_copy(row, owner)

            @pl.when(here)
            def _():
                pltpu.make_async_copy(owned.at[row, owner], place, r_out.at[tm]).start()

            @pl.when(jnp.logical_not(here))
            def _():
                copy.start()

    close = (x, left, right)

    @pl.when(driver)
    def _():
        for j in range(PARTS):
            centre(j)
            y_copy(1, 0, j, y, opposite).start()
            send_own(0, j)
        for j in range(PARTS):
            shift(y, j)
        neighbours(0, 0)
        pass_on(0, 0)
        neighbours(0, 1)
        pass_on(0, 1)
        neighbours(0, 2)
        for j in range(PARTS):
            arrived(2, j)
            send_own(1, j)
            if j == 0:
                neighbours(0, 3)
            if j == 2:
                for i in range(PARTS):
                    y_copy(0, 1, i, y, twin).start()
            if j >= 2:
                pass_far(0, j - 2)
            shift(across, j)
        pass_on(0, 2)
        pass_on(0, 3)
        multiply(y, close, True)
        multiply(across, (x,), False)
        send_terms(a, (x,))
        for j in range(PARTS):
            neighbours(1, j)
            pass_on(1, j)
        multiply(across, (left, right), False)
        send_terms(a, (left, right))
        pass_far(0, 2)
        pass_far(0, 3)
        multiply(y, (far,), True)
        for j in range(PARTS):
            arrived(0, j)
            shift(twin, j)
            if j == 1:
                pass_far(1, 0)
                pass_far(1, 1)
        multiply(twin, close + (far,), True)
        pass_far(1, 2)
        pass_far(1, 3)
        multiply(across, (far,), False)
        send_terms(a, (far,))
        send_out(a, close)
        for j in range(PARTS):
            arrived(1, j)
            shift(opposite, j)
            if j == 1:
                multiply(opposite, close + (far,), False, (0, 1))
            if j == 2:
                multiply(opposite, close + (far,), False, (2,))
        multiply(opposite, (x, left), False, (3,))
        send_terms(1 - a, (x, left))
        multiply(opposite, (right, far), False, (3,))
        send_terms(1 - a, (right, far))
        send_out(a, (far,))
        send_out(1 - a, close + (far,))

    @pl.when(jnp.logical_not(driver))
    def _():
        for j in range(PARTS):
            centre(j)
            y_copy(0, 0, j, y, twin).start()
        for j in range(PARTS):
            shift(y, j)
        for j in range(PARTS):
            arrived(0, j)
            y_copy(2, 2, j, twin, opposite).start()
            arrived(1, j)
            y_copy(2, 3, j, opposite, twin).start()
            shift(opposite, j)
            shift(twin, j)
        for j in range(PARTS):
            y_copy(1, 1, j, y, opposite).start()
        take(0, (0, 1, 2))
        multiply(y, close, True)
        multiply(twin, close, True)
        for j in range(PARTS):
            arrived(2, j)
            shift(across, j)
        take(1, (0,))
        multiply(opposite, (x,), False)
        send_terms(1 - a, (x,))
        multiply(across, (x,), False)
        send_terms(a, (x,))
        take(1, (1, 2))
        multiply(opposite, (left, right), False)
        send_terms(1 - a, (left, right))
        multiply(across, (left, right), False)
        send_terms(a, (left, right))
        take(0, (3,))
        multiply(y, (far,), True)
        multiply(twin, (far,), True)
        send_out(1 - a, (x,))
        send_out(a, (x,))
        take(1, (3,))
        multiply(opposite, (far,), False)
        send_terms(1 - a, (far,))
        multiply(across, (far,), False)
        send_terms(a, (far,))
        send_out(1 - a, (left, right))
        send_out(a, (left, right))
        send_out(1 - a, (far,))
        send_out(a, (far,))

    for slot in range(8):
        place = o_ref.at[slot // 2, :, pl.ds(128 * (slot % 2), 128)]
        pltpu.make_async_copy(owned.at[0, 0], place, r_out.at[slot]).wait()

    for i in range(1, 8):
        sum_copy(tm, (tm + i) & 7, i).wait_send()

    @pl.when(tm < 7)
    def _():
        halo_copy(tm + 1).wait_send()

    for j in range(PARTS):
        for group in range(2):
            y_copy(0, group, j, y, twin).wait_send()

    @pl.when(driver)
    def _():
        for q in range(2):
            for j in range(PARTS):
                for kind in range(3):
                    x_copy(q, kind, j, x, right).wait_send()
            for j in range(PARTS // 2):
                for kind in range(4):
                    sib_copy(q, kind, j).wait_send()

    @pl.when(jnp.logical_not(driver))
    def _():
        for j in range(PARTS):
            for group in range(2, 4):
                y_copy(0, group, j, y, twin).wait_send()

    for row in range(2):
        for owner in range(4):
            for i in range(1, 4):
                term_copy(row, owner, i).wait_send()
            here, place, copy = out_copy(row, owner)

            @pl.when(jnp.logical_not(here))
            def _():
                copy.wait_send()


def block(trajectory):
    rows = trajectory.shape[0]
    return pl.pallas_call(
        kernel,
        out_shape=jax.ShapeDtypeStruct((4, 128, 256), jnp.float32),
        in_specs=[pl.BlockSpec(memory_space=pl.ANY)],
        out_specs=pl.BlockSpec(memory_space=pl.ANY),
        scratch_shapes=[
            pltpu.VMEM((rows, 128), jnp.float32),
            pltpu.VMEM((8, 8, 128), jnp.float32),
            pltpu.VMEM((HALO, 128), jnp.float32),
            pltpu.VMEM((4, rows + HALO, 128), jnp.bfloat16),
            pltpu.VMEM((2, 4, 128, rows), jnp.bfloat16),
            pltpu.VMEM((4, rows, 512), jnp.bfloat16),
            pltpu.VMEM((2, 4, 4, 128, 128), jnp.float32),
            pltpu.VMEM((3, 2, 4, 128, 128), jnp.float32),
            pltpu.VMEM((2, 4, 128, 128), jnp.float32),
            pltpu.SemaphoreType.DMA,
            pltpu.SemaphoreType.DMA((8,)),
            pltpu.SemaphoreType.DMA((8,)),
            pltpu.SemaphoreType.DMA,
            pltpu.SemaphoreType.DMA,
            pltpu.SemaphoreType.DMA((4, PARTS)),
            pltpu.SemaphoreType.DMA((3, PARTS)),
            pltpu.SemaphoreType.DMA((2, 3, PARTS)),
            pltpu.SemaphoreType.DMA((2, 3, PARTS)),
            pltpu.SemaphoreType.DMA((2, 4, PARTS // 2)),
            pltpu.SemaphoreType.DMA((2, 4, PARTS // 2)),
            pltpu.SemaphoreType.DMA((3, 2, 4)),
            pltpu.SemaphoreType.DMA((3, 2, 4)),
            pltpu.SemaphoreType.DMA((2, 4)),
            pltpu.SemaphoreType.DMA((8,)),
        ],
        compiler_params=pltpu.CompilerParams(
            collective_id=0, has_side_effects=True, vmem_limit_bytes=52 << 20),
        cost_estimate=pl.CostEstimate(
            flops=2 * rows * 128 * 2048 * 4, bytes_accessed=3 << 20, transcendentals=0),
    )(trajectory)


def solution(mesh):
    return jax.shard_map(
        block, mesh=mesh, in_specs=(P("tm", "feat"),), out_specs=P(None, "feat", "tm"),
        check_vma=False)
```

```python
import functools
import math

import jax
import jax.numpy as jnp
from jax import lax
from jax.experimental import pallas as pl
from jax.experimental.pallas import tpu as pltpu
from jax.sharding import PartitionSpec as P

MESH = pl.DeviceIdType.MESH
LAGS = (0, 1, 4, 16)
HALO = 16
PARTS = 4


def device(x, y, z, c):
    return (z * 2 + (y >> 1), ((y & 1) * 4 + x) * 2 + c)


def kernel(
    x_hbm, o_ref, x_ref, sums, halo, slabs, cols, lagged, prod, terms, owned,
    s_in, s_sum, r_sum, s_halo, r_halo, s_y, r_y, s_x, r_x, s_sib, r_sib,
    s_term, r_term, s_out, r_out,
):
    rows = x_hbm.shape[0]
    part = rows // PARTS
    tm, feat = lax.axis_index("tm"), lax.axis_index("feat")
    c, x, a = feat & 1, (feat >> 1) & 3, feat >> 3
    z, h = tm >> 1, tm & 1
    y = h * 2 + a
    driver = c == h
    other = 1 - c
    twin = y + 1 - 2 * a
    opposite, across = (twin + 2) & 3, (y + 2) & 3
    left, right, far = (x + 3) & 3, (x + 1) & 3, (x + 2) & 3

    fetch = pltpu.make_async_copy(x_hbm, x_ref, s_in)
    fetch.start()

    barrier = pltpu.get_barrier_semaphore()

    def greet(*peer):
        pl.semaphore_signal(barrier, inc=1, device_id=peer, device_id_type=MESH)

    for i in (5, 3, 4, 7, 1, 6, 2):
        greet((tm + i) & 7, feat)
    for target in (twin, opposite):
        greet(*device(x, target, z, c))
    greet(*device(x, y, z, other))

    @pl.when(driver)
    def _():
        for target in (left, right):
            greet(*device(target, y, z, c))

    fetch.wait()
    total = jnp.zeros((8, 128), jnp.float32)
    for i in range(8):
        piece = x_ref[pl.ds(i * (rows // 8), rows // 8), :]
        total = total + jnp.sum(piece.reshape(rows // 64, 8, 128), axis=0)
    sums[tm] = total
    pl.semaphore_wait(barrier, jnp.where(driver, 12, 10))

    def sum_copy(slot, peer, i):
        return pltpu.make_async_remote_copy(
            src_ref=sums.at[slot], dst_ref=sums.at[slot], send_sem=s_sum.at[i],
            recv_sem=r_sum.at[slot], device_id=(peer, feat), device_id_type=MESH)

    def halo_copy(peer):
        return pltpu.make_async_remote_copy(
            src_ref=x_ref.at[pl.ds(rows - HALO, HALO)], dst_ref=halo, send_sem=s_halo,
            recv_sem=r_halo, device_id=(peer, feat), device_id_type=MESH)

    for i in (5, 3, 4, 7, 1, 6, 2):
        sum_copy(tm, (tm + i) & 7, i).start()

    @pl.when(tm < 7)
    def _():
        halo_copy(tm + 1).start()

    @pl.when(tm > 0)
    def _():
        halo_copy(tm - 1).wait_recv()

    @pl.when(tm == 0)
    def _():
        halo[...] = jnp.zeros_like(halo)

    for i in range(1, 8):
        sum_copy((tm + i) & 7, (tm + i) & 7, i).wait_recv()
    total = sums[0]
    for i in range(1, 8):
        total = total + sums[i]
    mean = jnp.sum(total, axis=0, keepdims=True) / (8.0 * rows)

    before = jnp.where(tm > 0, halo[...] - mean, 0.0)
    slabs[y, pl.ds(0, HALO), :] = before.astype(jnp.bfloat16)

    def centre(j):
        def body(i, carry):
            at = pl.multiple_of(part * j + i * 256, 256)
            value = x_ref[pl.ds(at, 256), :] - mean
            slabs[y, pl.ds(at + HALO, 256), :] = value.astype(jnp.bfloat16)
            return carry

        lax.fori_loop(0, part // 256, body, 0)

    def y_copy(kind, group, j, slab, target):
        at, size = (0, part + HALO) if j == 0 else (part * j + HALO, part)
        ref = slabs.at[slab, pl.ds(at, size)]
        return pltpu.make_async_remote_copy(
            src_ref=ref, dst_ref=ref, send_sem=s_y.at[group, j], recv_sem=r_y.at[kind, j],
            device_id=device(x, target, z, c), device_id_type=MESH)

    def arrived(kind, j):
        slab = (twin, opposite, across)[kind]
        y_copy(kind, 0, j, slab, twin).wait_recv()

    def half(q):
        return h if q == 0 else 1 - h

    def x_copy(q, kind, j, owner, target):
        ref = cols.at[half(q), owner, :, pl.ds(part * j, part)]
        return pltpu.make_async_remote_copy(
            src_ref=ref, dst_ref=ref, send_sem=s_x.at[q, kind, j], recv_sem=r_x.at[q, kind, j],
            device_id=device(target, y, z, c), device_id_type=MESH)

    def sib_copy(q, kind, j):
        owner = (x, left, right, far)[kind]
        ref = cols.at[half(q), owner, :, pl.ds(2 * part * j, 2 * part)]
        return pltpu.make_async_remote_copy(
            src_ref=ref, dst_ref=ref, send_sem=s_sib.at[q, kind, j], recv_sem=r_sib.at[q, kind, j],
            device_id=device(x, y, z, other), device_id_type=MESH)

    def send_own(q, j):
        slab = y if q == 0 else across
        value = slabs[slab, pl.ds(HALO + part * j, part), :]
        cols[half(q), x, :, pl.ds(part * j, part)] = value.T
        x_copy(q, 0, j, x, right).start()
        x_copy(q, 1, j, x, left).start()
        if j % 2:
            sib_copy(q, 0, j // 2).start()

    def neighbours(q, j):
        x_copy(q, 0, j, left, left).wait_recv()
        x_copy(q, 1, j, right, right).wait_recv()
        if j % 2:
            sib_copy(q, 1, j // 2).start()
            sib_copy(q, 2, j // 2).start()

    def pass_on(q, j):
        if j % 2 == 0:
            x_copy(q, 2, j, left, right).start()
        else:
            x_copy(q, 2, j, right, left).start()

    def pass_far(q, j):
        x_copy(q, 2, j, far, left).wait_recv()
        if j % 2:
            sib_copy(q, 3, j // 2).start()

    def take(q, kinds):
        for kind in kinds:
            for j in range(PARTS // 2):
                sib_copy(q, kind, j).wait_recv()

    def shift(slab, j):
        def body(i, carry):
            at = pl.multiple_of(part * j + i * 256, 256)
            raw = slabs[slab, pl.ds(at, 256 + HALO), :].astype(jnp.float32)
            for k, lag in enumerate(LAGS):
                moved = raw if lag == 0 else pltpu.roll(raw, lag, 0)
                lagged[slab, pl.ds(at, 256), 128 * k:128 * (k + 1)] = (
                    moved[HALO:, :].astype(jnp.bfloat16))
            return carry

        lax.fori_loop(0, part // 256, body, 0)

    def multiply(slab, owners, first, parts=None):
        at = pl.ds(0, rows) if parts is None else pl.ds(part * parts[0], part * len(parts))

        def body(n, carry):
            lanes = pl.ds(pl.multiple_of(n * 256, 256), 256)
            lhs = jnp.concatenate([cols[slab >> 1, owner, :, at] for owner in owners], axis=0)
            out = jnp.dot(lhs, lagged[slab, at, lanes], preferred_element_type=jnp.float32)
            for m, owner in enumerate(owners):
                for i in range(2):
                    block = out[128 * m:128 * (m + 1), 128 * i:128 * (i + 1)]
                    if not first:
                        block = prod[slab & 1, owner, 2 * n + i] + block
                    prod[slab & 1, owner, 2 * n + i] = block
            return carry

        lax.fori_loop(0, 2, body, 0)

    def term_copy(row, owner, i):
        target = (z + i) & 3
        return pltpu.make_async_remote_copy(
            src_ref=prod.at[row, owner, target], dst_ref=terms.at[i - 1, row, owner],
            send_sem=s_term.at[i - 1, row, owner], recv_sem=r_term.at[i - 1, row, owner],
            device_id=device(x, y, target, c), device_id_type=MESH)

    def send_terms(row, owners):
        for owner in owners:
            for i in (2, 1, 3):
                term_copy(row, owner, i).start()

    def out_copy(row, owner):
        ty, tz = 2 * (owner & 1) + row, 2 * a + (owner >> 1)
        place = o_ref.at[z, :, pl.ds(pl.multiple_of(h * 128, 128), 128)]
        copy = pltpu.make_async_remote_copy(
            src_ref=owned.at[row, owner], dst_ref=place, send_sem=s_out.at[row, owner],
            recv_sem=r_out.at[tm], device_id=device(x, ty, tz, c), device_id_type=MESH)
        return jnp.logical_and(ty == y, tz == z), place, copy

    scale = jnp.float32(1.0 / math.sqrt(8 * rows))
    for k in range(1, 4):
        scale = jnp.where(z == k, jnp.float32(1.0 / math.sqrt(8 * rows - LAGS[k])), scale)

    def send_out(row, owners):
        for owner in owners:
            value = prod[row, owner, z]
            for i in range(1, 4):
                term_copy(row, owner, i).wait_recv()
                value = value + terms[i - 1, row, owner]
            owned[row, owner] = value.T * scale
            here, place, copy = out_copy(row, owner)

            @pl.when(here)
            def _():
                pltpu.make_async_copy(owned.at[row, owner], place, r_out.at[tm]).start()

            @pl.when(jnp.logical_not(here))
            def _():
                copy.start()

    close = (x, left, right)

    @pl.when(driver)
    def _():
        for j in range(PARTS):
            centre(j)
            y_copy(1, 0, j, y, opposite).start()
            send_own(0, j)
        for j in range(PARTS):
            shift(y, j)
        neighbours(0, 0)
        pass_on(0, 0)
        neighbours(0, 1)
        pass_on(0, 1)
        neighbours(0, 2)
        for j in range(PARTS):
            arrived(2, j)
            send_own(1, j)
            if j == 0:
                neighbours(0, 3)
            if j == 2:
                for i in range(PARTS):
                    y_copy(0, 1, i, y, twin).start()
            if j >= 2:
                pass_far(0, j - 2)
            shift(across, j)
        pass_on(0, 2)
        pass_on(0, 3)
        multiply(y, close, True)
        multiply(across, (x,), False)
        send_terms(a, (x,))
        for j in range(PARTS):
            neighbours(1, j)
            pass_on(1, j)
        multiply(across, (left, right), False)
        send_terms(a, (left, right))
        pass_far(0, 2)
        pass_far(0, 3)
        multiply(y, (far,), True)
        send_out(a, (x,))
        for j in range(PARTS):
            arrived(0, j)
            shift(twin, j)
            if j == 1:
                pass_far(1, 0)
                pass_far(1, 1)
        multiply(twin, close + (far,), True)
        pass_far(1, 2)
        pass_far(1, 3)
        multiply(across, (far,), False)
        send_terms(a, (far,))
        send_out(a, (left, right))
        for j in range(PARTS):
            arrived(1, j)
            shift(opposite, j)
            if j == 1:
                multiply(opposite, close + (far,), False, (0, 1))
            if j == 2:
                multiply(opposite, close + (far,), False, (2,))
        multiply(opposite, (x, left), False, (3,))
        send_terms(1 - a, (x, left))
        multiply(opposite, (right, far), False, (3,))
        send_terms(1 - a, (right, far))
        send_out(a, (far,))
        send_out(1 - a, close + (far,))

    @pl.when(jnp.logical_not(driver))
    def _():
        for j in range(PARTS):
            centre(j)
            y_copy(0, 0, j, y, twin).start()
        for j in range(PARTS):
            shift(y, j)
        for j in range(PARTS):
            arrived(0, j)
            y_copy(2, 2, j, twin, opposite).start()
            arrived(1, j)
            y_copy(2, 3, j, opposite, twin).start()
            shift(opposite, j)
            shift(twin, j)
        for j in range(PARTS):
            y_copy(1, 1, j, y, opposite).start()
        take(0, (0, 1, 2))
        multiply(y, close, True)
        multiply(twin, close, True)
        take(1, (0,))
        multiply(opposite, (x,), False)
        send_terms(1 - a, (x,))
        for j in range(PARTS):
            arrived(2, j)
            shift(across, j)
        multiply(across, (x,), False)
        send_terms(a, (x,))
        take(1, (1, 2))
        multiply(opposite, (left, right), False)
        send_terms(1 - a, (left, right))
        multiply(across, (left, right), False)
        send_terms(a, (left, right))
        take(0, (3,))
        multiply(y, (far,), True)
        multiply(twin, (far,), True)
        take(1, (3,))
        multiply(opposite, (far,), False)
        send_terms(1 - a, (far,))
        multiply(across, (far,), False)
        send_terms(a, (far,))
        send_out(1 - a, close)
        send_out(a, close)
        send_out(1 - a, (far,))
        send_out(a, (far,))

    for i in range(1, 8):
        sum_copy(tm, (tm + i) & 7, i).wait_send()

    @pl.when(tm < 7)
    def _():
        halo_copy(tm + 1).wait_send()

    for j in range(PARTS):
        for group in range(2):
            y_copy(0, group, j, y, twin).wait_send()

    @pl.when(driver)
    def _():
        for q in range(2):
            for j in range(PARTS):
                for kind in range(3):
                    x_copy(q, kind, j, x, right).wait_send()
            for j in range(PARTS // 2):
                for kind in range(4):
                    sib_copy(q, kind, j).wait_send()

    @pl.when(jnp.logical_not(driver))
    def _():
        for j in range(PARTS):
            for group in range(2, 4):
                y_copy(0, group, j, y, twin).wait_send()

    for row in range(2):
        for owner in range(4):
            for i in range(1, 4):
                term_copy(row, owner, i).wait_send()
            here, place, copy = out_copy(row, owner)

            @pl.when(jnp.logical_not(here))
            def _():
                copy.wait_send()

    for slot in range(8):
        place = o_ref.at[slot // 2, :, pl.ds(128 * (slot % 2), 128)]
        pltpu.make_async_copy(owned.at[0, 0], place, r_out.at[slot]).wait()


def block(trajectory):
    rows = trajectory.shape[0]
    return pl.pallas_call(
        kernel,
        out_shape=jax.ShapeDtypeStruct((4, 128, 256), jnp.float32),
        in_specs=[pl.BlockSpec(memory_space=pl.ANY)],
        out_specs=pl.BlockSpec(memory_space=pl.ANY),
        scratch_shapes=[
            pltpu.VMEM((rows, 128), jnp.float32),
            pltpu.VMEM((8, 8, 128), jnp.float32),
            pltpu.VMEM((HALO, 128), jnp.float32),
            pltpu.VMEM((4, rows + HALO, 128), jnp.bfloat16),
            pltpu.VMEM((2, 4, 128, rows), jnp.bfloat16),
            pltpu.VMEM((4, rows, 512), jnp.bfloat16),
            pltpu.VMEM((2, 4, 4, 128, 128), jnp.float32),
            pltpu.VMEM((3, 2, 4, 128, 128), jnp.float32),
            pltpu.VMEM((2, 4, 128, 128), jnp.float32),
            pltpu.SemaphoreType.DMA,
            pltpu.SemaphoreType.DMA((8,)),
            pltpu.SemaphoreType.DMA((8,)),
            pltpu.SemaphoreType.DMA,
            pltpu.SemaphoreType.DMA,
            pltpu.SemaphoreType.DMA((4, PARTS)),
            pltpu.SemaphoreType.DMA((3, PARTS)),
            pltpu.SemaphoreType.DMA((2, 3, PARTS)),
            pltpu.SemaphoreType.DMA((2, 3, PARTS)),
            pltpu.SemaphoreType.DMA((2, 4, PARTS // 2)),
            pltpu.SemaphoreType.DMA((2, 4, PARTS // 2)),
            pltpu.SemaphoreType.DMA((3, 2, 4)),
            pltpu.SemaphoreType.DMA((3, 2, 4)),
            pltpu.SemaphoreType.DMA((2, 4)),
            pltpu.SemaphoreType.DMA((8,)),
        ],
        compiler_params=pltpu.CompilerParams(
            collective_id=0, has_side_effects=True, vmem_limit_bytes=52 << 20),
        cost_estimate=pl.CostEstimate(
            flops=2 * rows * 128 * 2048 * 4, bytes_accessed=3 << 20, transcendentals=0),
    )(trajectory)


def solution(mesh):
    return jax.shard_map(
        block, mesh=mesh, in_specs=(P("tm", "feat"),), out_specs=P(None, "feat", "tm"),
        check_vma=False)
```

```python
import functools
import math

import jax
import jax.numpy as jnp
from jax import lax
from jax.experimental import pallas as pl
from jax.experimental.pallas import tpu as pltpu
from jax.sharding import PartitionSpec as P

MESH = pl.DeviceIdType.MESH
LAGS = (0, 1, 4, 16)
HALO = 16
PARTS = 4


def device(x, y, z, c):
    return (z * 2 + (y >> 1), ((y & 1) * 4 + x) * 2 + c)


def kernel(
    x_hbm, o_ref, x_ref, sums, halo, slabs, cols, lagged, prod, terms, owned,
    s_in, s_sum, r_sum, s_halo, r_halo, s_y, r_y, s_x, r_x, s_sib, r_sib,
    s_term, r_term, s_out, r_out,
):
    rows = x_hbm.shape[0]
    part = rows // PARTS
    tm, feat = lax.axis_index("tm"), lax.axis_index("feat")
    c, x, a = feat & 1, (feat >> 1) & 3, feat >> 3
    z, h = tm >> 1, tm & 1
    y = h * 2 + a
    driver = c == h
    other = 1 - c
    twin = y + 1 - 2 * a
    opposite, across = (twin + 2) & 3, (y + 2) & 3
    left, right, far = (x + 3) & 3, (x + 1) & 3, (x + 2) & 3

    fetch = pltpu.make_async_copy(x_hbm, x_ref, s_in)
    fetch.start()

    barrier = pltpu.get_barrier_semaphore()

    def greet(*peer):
        pl.semaphore_signal(barrier, inc=1, device_id=peer, device_id_type=MESH)

    for i in (5, 3, 4, 7, 1, 6, 2):
        greet((tm + i) & 7, feat)
    for target in (twin, opposite):
        greet(*device(x, target, z, c))
    greet(*device(x, y, z, other))

    @pl.when(driver)
    def _():
        for target in (left, right):
            greet(*device(target, y, z, c))

    fetch.wait()
    total = jnp.zeros((8, 128), jnp.float32)
    for i in range(8):
        piece = x_ref[pl.ds(i * (rows // 8), rows // 8), :]
        total = total + jnp.sum(piece.reshape(rows // 64, 8, 128), axis=0)
    sums[tm] = total
    pl.semaphore_wait(barrier, jnp.where(driver, 12, 10))

    def sum_copy(slot, peer, i):
        return pltpu.make_async_remote_copy(
            src_ref=sums.at[slot], dst_ref=sums.at[slot], send_sem=s_sum.at[i],
            recv_sem=r_sum.at[slot], device_id=(peer, feat), device_id_type=MESH)

    def halo_copy(peer):
        return pltpu.make_async_remote_copy(
            src_ref=x_ref.at[pl.ds(rows - HALO, HALO)], dst_ref=halo, send_sem=s_halo,
            recv_sem=r_halo, device_id=(peer, feat), device_id_type=MESH)

    for i in (5, 3, 4, 7, 1, 6, 2):
        sum_copy(tm, (tm + i) & 7, i).start()

    @pl.when(tm < 7)
    def _():
        halo_copy(tm + 1).start()

    @pl.when(tm > 0)
    def _():
        halo_copy(tm - 1).wait_recv()

    @pl.when(tm == 0)
    def _():
        halo[...] = jnp.zeros_like(halo)

    for i in range(1, 8):
        sum_copy((tm + i) & 7, (tm + i) & 7, i).wait_recv()
    total = sums[0]
    for i in range(1, 8):
        total = total + sums[i]
    mean = jnp.sum(total, axis=0, keepdims=True) / (8.0 * rows)

    before = jnp.where(tm > 0, halo[...] - mean, 0.0)
    slabs[y, pl.ds(0, HALO), :] = before.astype(jnp.bfloat16)

    def centre(j):
        def body(i, carry):
            at = pl.multiple_of(part * j + i * 256, 256)
            value = x_ref[pl.ds(at, 256), :] - mean
            slabs[y, pl.ds(at + HALO, 256), :] = value.astype(jnp.bfloat16)
            return carry

        lax.fori_loop(0, part // 256, body, 0)

    def y_copy(kind, group, j, slab, target):
        at, size = (0, part + HALO) if j == 0 else (part * j + HALO, part)
        ref = slabs.at[slab, pl.ds(at, size)]
        return pltpu.make_async_remote_copy(
            src_ref=ref, dst_ref=ref, send_sem=s_y.at[group, j], recv_sem=r_y.at[kind, j],
            device_id=device(x, target, z, c), device_id_type=MESH)

    def arrived(kind, j):
        slab = (twin, opposite, across)[kind]
        y_copy(kind, 0, j, slab, twin).wait_recv()

    def half(q):
        return h if q == 0 else 1 - h

    def x_copy(q, kind, j, owner, target):
        ref = cols.at[half(q), owner, :, pl.ds(part * j, part)]
        return pltpu.make_async_remote_copy(
            src_ref=ref, dst_ref=ref, send_sem=s_x.at[q, kind, j], recv_sem=r_x.at[q, kind, j],
            device_id=device(target, y, z, c), device_id_type=MESH)

    def sib_copy(q, kind, j):
        owner = (x, left, right, far)[kind]
        ref = cols.at[half(q), owner, :, pl.ds(2 * part * j, 2 * part)]
        return pltpu.make_async_remote_copy(
            src_ref=ref, dst_ref=ref, send_sem=s_sib.at[q, kind, j], recv_sem=r_sib.at[q, kind, j],
            device_id=device(x, y, z, other), device_id_type=MESH)

    def send_own(q, j):
        slab = y if q == 0 else across
        value = slabs[slab, pl.ds(HALO + part * j, part), :]
        cols[half(q), x, :, pl.ds(part * j, part)] = value.T
        x_copy(q, 0, j, x, right).start()
        x_copy(q, 1, j, x, left).start()
        if j % 2:
            sib_copy(q, 0, j // 2).start()

    def neighbours(q, j):
        x_copy(q, 0, j, left, left).wait_recv()
        x_copy(q, 1, j, right, right).wait_recv()
        if j % 2:
            sib_copy(q, 1, j // 2).start()
            sib_copy(q, 2, j // 2).start()

    def pass_on(q, j):
        if j % 2 == 0:
            x_copy(q, 2, j, left, right).start()
        else:
            x_copy(q, 2, j, right, left).start()

    def pass_far(q, j):
        x_copy(q, 2, j, far, left).wait_recv()
        if j % 2:
            sib_copy(q, 3, j // 2).start()

    def take(q, kinds):
        for kind in kinds:
            for j in range(PARTS // 2):
                sib_copy(q, kind, j).wait_recv()

    def shift(slab, j):
        def body(i, carry):
            at = pl.multiple_of(part * j + i * 256, 256)
            raw = slabs[slab, pl.ds(at, 256 + HALO), :].astype(jnp.float32)
            for k, lag in enumerate(LAGS):
                if lag % HALO == 0:
                    moved = slabs[slab, pl.ds(at + HALO - lag, 256), :]
                else:
                    moved = pltpu.roll(raw, lag, 0)[HALO:, :].astype(jnp.bfloat16)
                lagged[slab, pl.ds(at, 256), 128 * k:128 * (k + 1)] = moved
            return carry

        lax.fori_loop(0, part // 256, body, 0)

    def multiply(slab, owners, first, parts=None):
        at = pl.ds(0, rows) if parts is None else pl.ds(part * parts[0], part * len(parts))

        def body(n, carry):
            lanes = pl.ds(pl.multiple_of(n * 256, 256), 256)
            lhs = jnp.concatenate([cols[slab >> 1, owner, :, at] for owner in owners], axis=0)
            out = jnp.dot(lhs, lagged[slab, at, lanes], preferred_element_type=jnp.float32)
            for m, owner in enumerate(owners):
                for i in range(2):
                    block = out[128 * m:128 * (m + 1), 128 * i:128 * (i + 1)]
                    if not first:
                        block = prod[slab & 1, owner, 2 * n + i] + block
                    prod[slab & 1, owner, 2 * n + i] = block
            return carry

        lax.fori_loop(0, 2, body, 0)

    def term_copy(row, owner, i):
        target = (z + i) & 3
        return pltpu.make_async_remote_copy(
            src_ref=prod.at[row, owner, target], dst_ref=terms.at[i - 1, row, owner],
            send_sem=s_term.at[i - 1, row, owner], recv_sem=r_term.at[i - 1, row, owner],
            device_id=device(x, y, target, c), device_id_type=MESH)

    def send_terms(row, owners):
        for owner in owners:
            for i in (2, 1, 3):
                term_copy(row, owner, i).start()

    def out_copy(row, owner):
        ty, tz = 2 * (owner & 1) + row, 2 * a + (owner >> 1)
        place = o_ref.at[z, :, pl.ds(pl.multiple_of(h * 128, 128), 128)]
        copy = pltpu.make_async_remote_copy(
            src_ref=owned.at[row, owner], dst_ref=place, send_sem=s_out.at[row, owner],
            recv_sem=r_out.at[tm], device_id=device(x, ty, tz, c), device_id_type=MESH)
        return jnp.logical_and(ty == y, tz == z), place, copy

    scale = jnp.float32(1.0 / math.sqrt(8 * rows))
    for k in range(1, 4):
        scale = jnp.where(z == k, jnp.float32(1.0 / math.sqrt(8 * rows - LAGS[k])), scale)

    def send_out(row, owners):
        for owner in owners:
            value = prod[row, owner, z]
            for i in range(1, 4):
                term_copy(row, owner, i).wait_recv()
                value = value + terms[i - 1, row, owner]
            owned[row, owner] = value.T * scale
            here, place, copy = out_copy(row, owner)

            @pl.when(here)
            def _():
                pltpu.make_async_copy(owned.at[row, owner], place, r_out.at[tm]).start()

            @pl.when(jnp.logical_not(here))
            def _():
                copy.start()

    close = (x, left, right)

    @pl.when(driver)
    def _():
        for j in range(PARTS):
            centre(j)
            y_copy(1, 0, j, y, opposite).start()
            send_own(0, j)
        for j in range(PARTS):
            shift(y, j)
        neighbours(0, 0)
        pass_on(0, 0)
        neighbours(0, 1)
        pass_on(0, 1)
        neighbours(0, 2)
        for j in range(PARTS):
            arrived(2, j)
            send_own(1, j)
            if j == 0:
                neighbours(0, 3)
            if j == 2:
                for i in range(PARTS):
                    y_copy(0, 1, i, y, twin).start()
            if j >= 2:
                pass_far(0, j - 2)
            shift(across, j)
        pass_on(0, 2)
        pass_on(0, 3)
        multiply(y, close, True)
        multiply(across, (x,), False)
        send_terms(a, (x,))
        for j in range(PARTS):
            neighbours(1, j)
            pass_on(1, j)
        multiply(across, (left, right), False)
        send_terms(a, (left, right))
        pass_far(0, 2)
        pass_far(0, 3)
        multiply(y, (far,), True)
        send_out(a, (x,))
        for j in range(PARTS):
            arrived(0, j)
            shift(twin, j)
            if j == 1:
                pass_far(1, 0)
                pass_far(1, 1)
        multiply(twin, close + (far,), True)
        pass_far(1, 2)
        pass_far(1, 3)
        multiply(across, (far,), False)
        send_terms(a, (far,))
        send_out(a, (left, right))
        for j in range(PARTS):
            arrived(1, j)
            shift(opposite, j)
            if j == 1:
                multiply(opposite, close + (far,), False, (0, 1))
            if j == 2:
                multiply(opposite, close + (far,), False, (2,))
        multiply(opposite, (x, left), False, (3,))
        send_terms(1 - a, (x, left))
        multiply(opposite, (right, far), False, (3,))
        send_terms(1 - a, (right, far))
        send_out(a, (far,))
        send_out(1 - a, close + (far,))

    @pl.when(jnp.logical_not(driver))
    def _():
        for j in range(PARTS):
            centre(j)
            y_copy(0, 0, j, y, twin).start()
        for j in range(PARTS):
            shift(y, j)
        for j in range(PARTS):
            arrived(0, j)
            y_copy(2, 2, j, twin, opposite).start()
            arrived(1, j)
            y_copy(2, 3, j, opposite, twin).start()
            shift(opposite, j)
            shift(twin, j)
        for j in range(PARTS):
            y_copy(1, 1, j, y, opposite).start()
        take(0, (0, 1, 2))
        multiply(y, close, True)
        multiply(twin, close, True)
        take(1, (0,))
        multiply(opposite, (x,), False)
        send_terms(1 - a, (x,))
        for j in range(PARTS):
            arrived(2, j)
            shift(across, j)
        multiply(across, (x,), False)
        send_terms(a, (x,))
        take(1, (1, 2))
        multiply(opposite, (left, right), False)
        send_terms(1 - a, (left, right))
        multiply(across, (left, right), False)
        send_terms(a, (left, right))
        take(0, (3,))
        multiply(y, (far,), True)
        multiply(twin, (far,), True)
        take(1, (3,))
        multiply(opposite, (far,), False)
        send_terms(1 - a, (far,))
        multiply(across, (far,), False)
        send_terms(a, (far,))
        send_out(1 - a, close)
        send_out(a, close)
        send_out(1 - a, (far,))
        send_out(a, (far,))

    for i in range(1, 8):
        sum_copy(tm, (tm + i) & 7, i).wait_send()

    @pl.when(tm < 7)
    def _():
        halo_copy(tm + 1).wait_send()

    for j in range(PARTS):
        for group in range(2):
            y_copy(0, group, j, y, twin).wait_send()

    @pl.when(driver)
    def _():
        for q in range(2):
            for j in range(PARTS):
                for kind in range(3):
                    x_copy(q, kind, j, x, right).wait_send()
            for j in range(PARTS // 2):
                for kind in range(4):
                    sib_copy(q, kind, j).wait_send()

    @pl.when(jnp.logical_not(driver))
    def _():
        for j in range(PARTS):
            for group in range(2, 4):
                y_copy(0, group, j, y, twin).wait_send()

    for row in range(2):
        for owner in range(4):
            for i in range(1, 4):
                term_copy(row, owner, i).wait_send()
            here, place, copy = out_copy(row, owner)

            @pl.when(jnp.logical_not(here))
            def _():
                copy.wait_send()

    for slot in range(8):
        place = o_ref.at[slot // 2, :, pl.ds(128 * (slot % 2), 128)]
        pltpu.make_async_copy(owned.at[0, 0], place, r_out.at[slot]).wait()


def block(trajectory):
    rows = trajectory.shape[0]
    return pl.pallas_call(
        kernel,
        out_shape=jax.ShapeDtypeStruct((4, 128, 256), jnp.float32),
        in_specs=[pl.BlockSpec(memory_space=pl.ANY)],
        out_specs=pl.BlockSpec(memory_space=pl.ANY),
        scratch_shapes=[
            pltpu.VMEM((rows, 128), jnp.float32),
            pltpu.VMEM((8, 8, 128), jnp.float32),
            pltpu.VMEM((HALO, 128), jnp.float32),
            pltpu.VMEM((4, rows + HALO, 128), jnp.bfloat16),
            pltpu.VMEM((2, 4, 128, rows), jnp.bfloat16),
            pltpu.VMEM((4, rows, 512), jnp.bfloat16),
            pltpu.VMEM((2, 4, 4, 128, 128), jnp.float32),
            pltpu.VMEM((3, 2, 4, 128, 128), jnp.float32),
            pltpu.VMEM((2, 4, 128, 128), jnp.float32),
            pltpu.SemaphoreType.DMA,
            pltpu.SemaphoreType.DMA((8,)),
            pltpu.SemaphoreType.DMA((8,)),
            pltpu.SemaphoreType.DMA,
            pltpu.SemaphoreType.DMA,
            pltpu.SemaphoreType.DMA((4, PARTS)),
            pltpu.SemaphoreType.DMA((3, PARTS)),
            pltpu.SemaphoreType.DMA((2, 3, PARTS)),
            pltpu.SemaphoreType.DMA((2, 3, PARTS)),
            pltpu.SemaphoreType.DMA((2, 4, PARTS // 2)),
            pltpu.SemaphoreType.DMA((2, 4, PARTS // 2)),
            pltpu.SemaphoreType.DMA((3, 2, 4)),
            pltpu.SemaphoreType.DMA((3, 2, 4)),
            pltpu.SemaphoreType.DMA((2, 4)),
            pltpu.SemaphoreType.DMA((8,)),
        ],
        compiler_params=pltpu.CompilerParams(
            collective_id=0, has_side_effects=True, vmem_limit_bytes=52 << 20),
        cost_estimate=pl.CostEstimate(
            flops=2 * rows * 128 * 2048 * 4, bytes_accessed=3 << 20, transcendentals=0),
    )(trajectory)


def solution(mesh):
    return jax.shard_map(
        block, mesh=mesh, in_specs=(P("tm", "feat"),), out_specs=P(None, "feat", "tm"),
        check_vma=False)
```

```python
import functools
import math

import jax
import jax.numpy as jnp
from jax import lax
from jax.experimental import pallas as pl
from jax.experimental.pallas import tpu as pltpu
from jax.sharding import PartitionSpec as P

MESH = pl.DeviceIdType.MESH
LAGS = (0, 1, 4, 16)
HALO = 16
PARTS = 4


def device(x, y, z, c):
    return (z * 2 + (y >> 1), ((y & 1) * 4 + x) * 2 + c)


def kernel(
    x_hbm, o_ref, x_ref, sums, halo, slabs, cols, lagged, prod, terms, owned,
    s_in, s_sum, r_sum, s_halo, r_halo, s_y, r_y, s_x, r_x, s_sib, r_sib,
    s_term, r_term, s_out, r_out,
):
    rows = x_hbm.shape[0]
    part = rows // PARTS
    tm, feat = lax.axis_index("tm"), lax.axis_index("feat")
    c, x, a = feat & 1, (feat >> 1) & 3, feat >> 3
    z, h = tm >> 1, tm & 1
    y = h * 2 + a
    driver = c == h
    other = 1 - c
    twin = y + 1 - 2 * a
    opposite, across = (twin + 2) & 3, (y + 2) & 3
    left, right, far = (x + 3) & 3, (x + 1) & 3, (x + 2) & 3

    fetch = pltpu.make_async_copy(x_hbm, x_ref, s_in)
    fetch.start()

    barrier = pltpu.get_barrier_semaphore()

    def greet(*peer):
        pl.semaphore_signal(barrier, inc=1, device_id=peer, device_id_type=MESH)

    for i in (5, 3, 4, 7, 1, 6, 2):
        greet((tm + i) & 7, feat)
    for target in (twin, opposite):
        greet(*device(x, target, z, c))
    greet(*device(x, y, z, other))

    @pl.when(driver)
    def _():
        for target in (left, right):
            greet(*device(target, y, z, c))

    fetch.wait()
    total = jnp.zeros((8, 128), jnp.float32)
    for i in range(8):
        piece = x_ref[pl.ds(i * (rows // 8), rows // 8), :]
        total = total + jnp.sum(piece.reshape(rows // 64, 8, 128), axis=0)
    sums[tm] = total
    pl.semaphore_wait(barrier, jnp.where(driver, 12, 10))

    def sum_copy(slot, peer, i):
        return pltpu.make_async_remote_copy(
            src_ref=sums.at[slot], dst_ref=sums.at[slot], send_sem=s_sum.at[i],
            recv_sem=r_sum.at[slot], device_id=(peer, feat), device_id_type=MESH)

    def halo_copy(peer):
        return pltpu.make_async_remote_copy(
            src_ref=x_ref.at[pl.ds(rows - HALO, HALO)], dst_ref=halo, send_sem=s_halo,
            recv_sem=r_halo, device_id=(peer, feat), device_id_type=MESH)

    for i in (5, 3, 4, 7, 1, 6, 2):
        sum_copy(tm, (tm + i) & 7, i).start()

    @pl.when(tm < 7)
    def _():
        halo_copy(tm + 1).start()

    @pl.when(tm > 0)
    def _():
        halo_copy(tm - 1).wait_recv()

    @pl.when(tm == 0)
    def _():
        halo[...] = jnp.zeros_like(halo)

    for i in range(1, 8):
        sum_copy((tm + i) & 7, (tm + i) & 7, i).wait_recv()
    total = sums[0]
    for i in range(1, 8):
        total = total + sums[i]
    mean = jnp.sum(total, axis=0, keepdims=True) / (8.0 * rows)

    before = jnp.where(tm > 0, halo[...] - mean, 0.0)
    slabs[y, pl.ds(0, HALO), :] = before.astype(jnp.bfloat16)

    def centre(j):
        def body(i, carry):
            at = pl.multiple_of(part * j + i * 256, 256)
            value = x_ref[pl.ds(at, 256), :] - mean
            slabs[y, pl.ds(at + HALO, 256), :] = value.astype(jnp.bfloat16)
            return carry

        lax.fori_loop(0, part // 256, body, 0)

    def y_copy(kind, group, j, slab, target):
        at, size = (0, part + HALO) if j == 0 else (part * j + HALO, part)
        ref = slabs.at[slab, pl.ds(at, size)]
        return pltpu.make_async_remote_copy(
            src_ref=ref, dst_ref=ref, send_sem=s_y.at[group, j], recv_sem=r_y.at[kind, j],
            device_id=device(x, target, z, c), device_id_type=MESH)

    def arrived(kind, j):
        slab = (twin, opposite, across)[kind]
        y_copy(kind, 0, j, slab, twin).wait_recv()

    def half(q):
        return h if q == 0 else 1 - h

    def x_copy(q, kind, j, owner, target):
        ref = cols.at[half(q), owner, :, pl.ds(part * j, part)]
        return pltpu.make_async_remote_copy(
            src_ref=ref, dst_ref=ref, send_sem=s_x.at[q, kind, j], recv_sem=r_x.at[q, kind, j],
            device_id=device(target, y, z, c), device_id_type=MESH)

    def sib_copy(q, kind, j):
        owner = (x, left, right, far)[kind]
        ref = cols.at[half(q), owner, :, pl.ds(2 * part * j, 2 * part)]
        return pltpu.make_async_remote_copy(
            src_ref=ref, dst_ref=ref, send_sem=s_sib.at[q, kind, j], recv_sem=r_sib.at[q, kind, j],
            device_id=device(x, y, z, other), device_id_type=MESH)

    def send_own(q, j):
        slab = y if q == 0 else across
        value = slabs[slab, pl.ds(HALO + part * j, part), :]
        cols[half(q), x, :, pl.ds(part * j, part)] = value.T
        x_copy(q, 0, j, x, right).start()
        x_copy(q, 1, j, x, left).start()
        if j % 2:
            sib_copy(q, 0, j // 2).start()

    def neighbours(q, j):
        x_copy(q, 0, j, left, left).wait_recv()
        x_copy(q, 1, j, right, right).wait_recv()
        if j % 2:
            sib_copy(q, 1, j // 2).start()
            sib_copy(q, 2, j // 2).start()

    def pass_on(q, j):
        if j % 2 == 0:
            x_copy(q, 2, j, left, right).start()
        else:
            x_copy(q, 2, j, right, left).start()

    def pass_far(q, j):
        x_copy(q, 2, j, far, left).wait_recv()
        if j % 2:
            sib_copy(q, 3, j // 2).start()

    def take(q, kinds):
        for kind in kinds:
            for j in range(PARTS // 2):
                sib_copy(q, kind, j).wait_recv()

    def shift(slab, j):
        def body(i, carry):
            at = pl.multiple_of(part * j + i * 256, 256)
            raw = slabs[slab, pl.ds(at, 256 + HALO), :].astype(jnp.float32)
            for k, lag in enumerate(LAGS):
                moved = raw if lag == 0 else pltpu.roll(raw, lag, 0)
                lagged[slab, pl.ds(at, 256), 128 * k:128 * (k + 1)] = (
                    moved[HALO:, :].astype(jnp.bfloat16))
            return carry

        lax.fori_loop(0, part // 256, body, 0)

    def multiply(slab, owners, first, parts=None):
        at = pl.ds(0, rows) if parts is None else pl.ds(part * parts[0], part * len(parts))

        def body(n, carry):
            lanes = pl.ds(pl.multiple_of(n * 256, 256), 256)
            lhs = jnp.concatenate([cols[slab >> 1, owner, :, at] for owner in owners], axis=0)
            out = jnp.dot(lhs, lagged[slab, at, lanes], preferred_element_type=jnp.float32)
            for m, owner in enumerate(owners):
                for i in range(2):
                    block = out[128 * m:128 * (m + 1), 128 * i:128 * (i + 1)]
                    if not first:
                        block = prod[slab & 1, owner, 2 * n + i] + block
                    prod[slab & 1, owner, 2 * n + i] = block
            return carry

        lax.fori_loop(0, 2, body, 0)

    def term_copy(row, owner, i):
        target = (z + i) & 3
        return pltpu.make_async_remote_copy(
            src_ref=prod.at[row, owner, target], dst_ref=terms.at[i - 1, row, owner],
            send_sem=s_term.at[i - 1, row, owner], recv_sem=r_term.at[i - 1, row, owner],
            device_id=device(x, y, target, c), device_id_type=MESH)

    def send_terms(row, owners):
        for owner in owners:
            for i in (2, 1, 3):
                term_copy(row, owner, i).start()

    def out_copy(row, owner):
        ty, tz = 2 * (owner & 1) + row, 2 * a + (owner >> 1)
        place = o_ref.at[z, :, pl.ds(pl.multiple_of(h * 128, 128), 128)]
        copy = pltpu.make_async_remote_copy(
            src_ref=owned.at[row, owner], dst_ref=place, send_sem=s_out.at[row, owner],
            recv_sem=r_out.at[tm], device_id=device(x, ty, tz, c), device_id_type=MESH)
        return jnp.logical_and(ty == y, tz == z), place, copy

    scale = jnp.float32(1.0 / math.sqrt(8 * rows))
    for k in range(1, 4):
        scale = jnp.where(z == k, jnp.float32(1.0 / math.sqrt(8 * rows - LAGS[k])), scale)

    def send_out(row, owners):
        for owner in owners:
            value = prod[row, owner, z]
            for i in range(1, 4):
                term_copy(row, owner, i).wait_recv()
                value = value + terms[i - 1, row, owner]
            owned[row, owner] = value.T * scale
            here, place, copy = out_copy(row, owner)

            @pl.when(here)
            def _():
                pltpu.make_async_copy(owned.at[row, owner], place, r_out.at[tm]).start()

            @pl.when(jnp.logical_not(here))
            def _():
                copy.start()

    close = (x, left, right)

    @pl.when(driver)
    def _():
        for j in range(PARTS):
            centre(j)
            send_own(0, j)
            y_copy(1, 0, j, y, opposite).start()
        for j in range(PARTS):
            shift(y, j)
        neighbours(0, 0)
        pass_on(0, 0)
        neighbours(0, 1)
        pass_on(0, 1)
        neighbours(0, 2)
        for j in range(PARTS):
            arrived(2, j)
            send_own(1, j)
            if j == 0:
                neighbours(0, 3)
            if j == 2:
                for i in range(PARTS):
                    y_copy(0, 1, i, y, twin).start()
            if j >= 2:
                pass_far(0, j - 2)
            shift(across, j)
        pass_on(0, 2)
        pass_on(0, 3)
        multiply(y, close, True)
        multiply(across, (x,), False)
        send_terms(a, (x,))
        for j in range(PARTS):
            neighbours(1, j)
            pass_on(1, j)
        multiply(across, (left, right), False)
        send_terms(a, (left, right))
        pass_far(0, 2)
        pass_far(0, 3)
        multiply(y, (far,), True)
        send_out(a, (x,))
        for j in range(PARTS):
            arrived(0, j)
            shift(twin, j)
            if j == 1:
                pass_far(1, 0)
                pass_far(1, 1)
        multiply(twin, close + (far,), True)
        pass_far(1, 2)
        pass_far(1, 3)
        multiply(across, (far,), False)
        send_terms(a, (far,))
        send_out(a, (left, right))
        for j in range(PARTS):
            arrived(1, j)
            shift(opposite, j)
            if j == 1:
                multiply(opposite, close + (far,), False, (0, 1))
            if j == 2:
                multiply(opposite, close + (far,), False, (2,))
        multiply(opposite, (x, left), False, (3,))
        send_terms(1 - a, (x, left))
        multiply(opposite, (right, far), False, (3,))
        send_terms(1 - a, (right, far))
        send_out(a, (far,))
        send_out(1 - a, close + (far,))

    @pl.when(jnp.logical_not(driver))
    def _():
        for j in range(PARTS):
            centre(j)
            y_copy(0, 0, j, y, twin).start()
        for j in range(PARTS):
            shift(y, j)
        for j in range(PARTS):
            arrived(0, j)
            y_copy(2, 2, j, twin, opposite).start()
            arrived(1, j)
            y_copy(2, 3, j, opposite, twin).start()
            shift(opposite, j)
            shift(twin, j)
        for j in range(PARTS):
            y_copy(1, 1, j, y, opposite).start()
        take(0, (0, 1, 2))
        multiply(y, close, True)
        multiply(twin, close, True)
        take(1, (0,))
        multiply(opposite, (x,), False)
        send_terms(1 - a, (x,))
        for j in range(PARTS):
            arrived(2, j)
            shift(across, j)
        multiply(across, (x,), False)
        send_terms(a, (x,))
        take(1, (1, 2))
        multiply(opposite, (left, right), False)
        send_terms(1 - a, (left, right))
        multiply(across, (left, right), False)
        send_terms(a, (left, right))
        take(0, (3,))
        multiply(y, (far,), True)
        multiply(twin, (far,), True)
        take(1, (3,))
        multiply(opposite, (far,), False)
        send_terms(1 - a, (far,))
        multiply(across, (far,), False)
        send_terms(a, (far,))
        send_out(1 - a, close)
        send_out(a, close)
        send_out(1 - a, (far,))
        send_out(a, (far,))

    for i in range(1, 8):
        sum_copy(tm, (tm + i) & 7, i).wait_send()

    @pl.when(tm < 7)
    def _():
        halo_copy(tm + 1).wait_send()

    for j in range(PARTS):
        for group in range(2):
            y_copy(0, group, j, y, twin).wait_send()

    @pl.when(driver)
    def _():
        for q in range(2):
            for j in range(PARTS):
                for kind in range(3):
                    x_copy(q, kind, j, x, right).wait_send()
            for j in range(PARTS // 2):
                for kind in range(4):
                    sib_copy(q, kind, j).wait_send()

    @pl.when(jnp.logical_not(driver))
    def _():
        for j in range(PARTS):
            for group in range(2, 4):
                y_copy(0, group, j, y, twin).wait_send()

    for row in range(2):
        for owner in range(4):
            for i in range(1, 4):
                term_copy(row, owner, i).wait_send()
            here, place, copy = out_copy(row, owner)

            @pl.when(jnp.logical_not(here))
            def _():
                copy.wait_send()

    for slot in range(8):
        place = o_ref.at[slot // 2, :, pl.ds(128 * (slot % 2), 128)]
        pltpu.make_async_copy(owned.at[0, 0], place, r_out.at[slot]).wait()


def block(trajectory):
    rows = trajectory.shape[0]
    return pl.pallas_call(
        kernel,
        out_shape=jax.ShapeDtypeStruct((4, 128, 256), jnp.float32),
        in_specs=[pl.BlockSpec(memory_space=pl.ANY)],
        out_specs=pl.BlockSpec(memory_space=pl.ANY),
        scratch_shapes=[
            pltpu.VMEM((rows, 128), jnp.float32),
            pltpu.VMEM((8, 8, 128), jnp.float32),
            pltpu.VMEM((HALO, 128), jnp.float32),
            pltpu.VMEM((4, rows + HALO, 128), jnp.bfloat16),
            pltpu.VMEM((2, 4, 128, rows), jnp.bfloat16),
            pltpu.VMEM((4, rows, 512), jnp.bfloat16),
            pltpu.VMEM((2, 4, 4, 128, 128), jnp.float32),
            pltpu.VMEM((3, 2, 4, 128, 128), jnp.float32),
            pltpu.VMEM((2, 4, 128, 128), jnp.float32),
            pltpu.SemaphoreType.DMA,
            pltpu.SemaphoreType.DMA((8,)),
            pltpu.SemaphoreType.DMA((8,)),
            pltpu.SemaphoreType.DMA,
            pltpu.SemaphoreType.DMA,
            pltpu.SemaphoreType.DMA((4, PARTS)),
            pltpu.SemaphoreType.DMA((3, PARTS)),
            pltpu.SemaphoreType.DMA((2, 3, PARTS)),
            pltpu.SemaphoreType.DMA((2, 3, PARTS)),
            pltpu.SemaphoreType.DMA((2, 4, PARTS // 2)),
            pltpu.SemaphoreType.DMA((2, 4, PARTS // 2)),
            pltpu.SemaphoreType.DMA((3, 2, 4)),
            pltpu.SemaphoreType.DMA((3, 2, 4)),
            pltpu.SemaphoreType.DMA((2, 4)),
            pltpu.SemaphoreType.DMA((8,)),
        ],
        compiler_params=pltpu.CompilerParams(
            collective_id=0, has_side_effects=True, vmem_limit_bytes=52 << 20),
        cost_estimate=pl.CostEstimate(
            flops=2 * rows * 128 * 2048 * 4, bytes_accessed=3 << 20, transcendentals=0),
    )(trajectory)


def solution(mesh):
    return jax.shard_map(
        block, mesh=mesh, in_specs=(P("tm", "feat"),), out_specs=P(None, "feat", "tm"),
        check_vma=False)
```
